256 devices in a mesh: lat: 8 (over y_lo, x), lon: 32 (over z, y_hi, core).
Axes of the slice: x: 4, y: 4 (y_hi: 2, y_lo: 2; y = y_hi * 2 + y_lo), z: 8, core: 2. Of those that a mesh axis runs over, the one named last changes fastest.
Arguments:
- tokens: bfloat16 [48, 1536, 192], P('lat', 'lon'), may hold values from -6 to 6
- norm1_gain: float32 [192], replicated, may hold values from 0.1 to 1.9
- qkv_weight: bfloat16 [192, 576], replicated, may hold values from -0.4375 to 0.4375
- bias_table: float32 [9, 6, 828], replicated, may hold values from -4 to 325
- bias_index: int32 [9, 5184], replicated, may hold values from 0 to 827
- region_ids: int32 [48], replicated, may hold values from 0 to 3, never falling along the last dimension, each value on 1 to 24 neighbouring positions
- proj_weight: bfloat16 [192, 192], replicated, may hold values from -0.4375 to 0.4375
- norm2_gain: float32 [192], replicated, may hold values from 0.1 to 1.9
- fc1_weight: bfloat16 [192, 768], replicated, may hold values from -0.4375 to 0.4375
- fc2_weight: bfloat16 [768, 192], replicated, may hold values from -0.21875 to 0.21875
- recover_weight: bfloat16 [192, 80], replicated, may hold values from -0.4375 to 0.4375
- cotangent: bfloat16 [5, 192, 6144], P(None, 'lat', 'lon'), may hold values from -6 to 6
Outputs:
- field: bfloat16 [5, 192, 6144], P(None, 'lat', 'lon')
- token_grad: bfloat16 [48, 1536, 192], P('lat', 'lon')
The draws below stay inside these ranges and needn't reach their ends.
Inputs may be any that keep to these rules, and one draw needn't show every extreme that they name: `region_ids`: region numbers never fall along latitude; a region covers 1 to 24 consecutive rows.
All inputs are finite; a program needn't handle non-finite values.
Results may differ from the reference program's by a relative error of at most 0.022.
Values may be sent and summed in bfloat16 or wider, within the bound.
A program may use at most 192 MiB of HBM per device.

```python
import math
import jax
import jax.numpy as jnp
import numpy as np
from jax import lax

C = 192
HEADS = 6
MLP = 768
VARS = 5
WLAT = 6
WLON = 12
SLOTS = 828
PAIRS = 5184
LATG = 48
LONG = 1536
NWR = 9
REGIONS = 4


def draw_bias_table(key, part):
    key = jax.random.fold_in(key, 7)
    first_key = jax.random.fold_in(key, 0)
    shape = (NWR, HEADS, SLOTS)
    return jnp.clip(jax.random.normal(first_key, shape), -4.0, 4.0).astype(jnp.float32)


def with_ends(entries, key, low, high):
    spot = [jax.random.randint(jax.random.fold_in(key, axis), (), 0, length) for axis, length in enumerate(entries.shape)]
    main_axis = entries.shape.index(max(entries.shape))
    neighbour = spot[:main_axis] + [(spot[main_axis] + 1) % entries.shape[main_axis]] + spot[main_axis + 1:]
    return entries.at[tuple(spot)].set(low).at[tuple(neighbour)].set(high)


def block_levels(stream_key, extent, shards, least, top_value):
    level = 1.0
    for axis_at, shards_of in shards:
        draws = jax.random.uniform(jax.random.fold_in(jax.random.fold_in(stream_key, 6), axis_at), (shards_of,), jnp.float32, least / len(shards), top_value / len(shards))
        level = level * jnp.repeat(jnp.exp(draws), extent[axis_at] // shards_of).reshape((-1,) + (1,) * (len(extent) - 1 - axis_at))
    return level


def split_up(count, total, limit, slope):
    portions = [(1 << 20) // math.isqrt(standing ** slope) + 1 for standing in range(2, count + 1)]
    surplus, counts = total - limit - (count - 1), [1] * (count - 1)
    while surplus > 0:
        candidates = [i for i in range(count - 1) if counts[i] < limit]
        pool, budget = sum([portions[i] for i in candidates]), surplus
        for i in candidates:
            more = min(limit - counts[i], max(1, budget * portions[i] // pool), surplus)
            counts[i] = counts[i] + more
            surplus = surplus - more
    return np.array([limit] + counts)


def ragged(own_key, count, total, reach, lean):
    if count == 2:
        one = jax.random.randint(own_key, (), max(1, total - reach), min(reach, total - 1) + 1)
        return jnp.stack([one, total - one])
    tallies = jnp.asarray(split_up(count, total, reach, lean), jnp.int32)
    couples = (count - 1) // 2
    source_of, taker = tallies[1:1 + 2 * couples:2], tallies[2:2 + 2 * couples:2]
    margin = jnp.minimum(source_of - 1, reach - taker)
    passed = jax.random.randint(jax.random.fold_in(own_key, 1), (couples,), 0, 1 << 20) % (margin + 1)
    tallies = tallies.at[1:1 + 2 * couples:2].set(source_of - passed).at[2:2 + 2 * couples:2].set(taker + passed)
    return tallies[jax.random.permutation(jax.random.fold_in(own_key, 2), count)]


def gaussian(rng, shape, width, most, cuts=(), dtype=jnp.bfloat16):
    array = jax.random.normal(rng, shape, jnp.float32) * width
    if len(cuts) > 0:
        array = block_levels(rng, shape, cuts, -0.22, 0.18) * array
    return jnp.clip(array, min=-most, max=most).astype(dtype)


def setup_inputs(seed: int = 0) -> dict:
    key_list = jax.random.split(jax.random.key(seed), 13)
    return {
        "tokens": gaussian(key_list[0], (LATG, LONG, C), 1.0, 6.0, ((0, 8), (1, 32))),
        "norm1_gain": jnp.clip(1.0 + 0.18 * jax.random.normal(key_list[1], (C,), jnp.float32), 0.1, 1.9),
        "qkv_weight": gaussian(key_list[2], (C, 3 * C), C ** -0.5, 0.4375),
        "bias_table": draw_bias_table(jax.random.fold_in(key_list[12], 71), 0),
        "bias_index": with_ends(jax.random.randint(key_list[4], (NWR, PAIRS), 0, SLOTS), jax.random.fold_in(key_list[4], 1), 0, SLOTS - 1).astype(jnp.int32),
        "region_ids": jnp.searchsorted(jnp.cumsum(ragged(key_list[5], REGIONS, LATG, 24, 0)), jnp.arange(LATG), side="right").astype(jnp.int32),
        "proj_weight": gaussian(key_list[6], (C, C), C ** -0.5, 0.4375),
        "norm2_gain": jnp.clip(1.0 + 0.18 * jax.random.normal(key_list[7], (C,), jnp.float32), 0.1, 1.9),
        "fc1_weight": gaussian(key_list[8], (C, MLP), C ** -0.5, 0.4375),
        "fc2_weight": gaussian(key_list[9], (MLP, C), MLP ** -0.5, 0.21875),
        "recover_weight": gaussian(key_list[10], (C, 16 * VARS), C ** -0.5, 0.4375),
        "cotangent": gaussian(key_list[11], (VARS, 4 * LATG, 4 * LONG), 1.0, 6.0, ((1, 8), (2, 32))),
    }


epsilon = 1e-05

def layer_norm(inputs, gain):
    values = inputs.astype(jnp.float32)
    average = lax.optimization_barrier(jnp.mean(values, axis=-1, keepdims=True))
    centered = values - average
    spread = lax.optimization_barrier(jnp.mean(centered * centered, axis=-1, keepdims=True))
    return centered * lax.rsqrt(spread + epsilon) * gain

def prepare(inputs, norm1_gain, qkv_weight):
    normed = layer_norm(inputs, norm1_gain).astype(jnp.bfloat16)
    return jnp.dot(normed, qkv_weight, preferred_element_type=jnp.float32).astype(jnp.bfloat16)

def window_bias(bias_rows, pair_index):
    picked = jnp.take_along_axis(bias_rows, pair_index[:, None, :], axis=2)
    side = WLAT * WLON
    return picked.reshape(bias_rows.shape[0], bias_rows.shape[1], side, side)

def window_mask(regions):
    token_region = jnp.repeat(regions, WLON, axis=1)
    return token_region[:, :, None] == token_region[:, None, :]

def attend(projected, pair_bias, allowed):
    window_rows, height, tile_span, triple = projected.shape
    head_count = pair_bias.shape[1]
    channels = triple // 3
    head_depth = channels // head_count
    blocks = tile_span // WLON
    grouped = projected.reshape(window_rows, height, blocks, WLON, 3, head_count, head_depth)
    grouped = grouped.transpose(0, 2, 1, 3, 4, 5, 6).reshape(window_rows, blocks, height * WLON, 3, head_count, head_depth)
    queries = grouped[:, :, :, 0].astype(jnp.float32)
    key_vectors = grouped[:, :, :, 1].astype(jnp.float32)
    values = grouped[:, :, :, 2].astype(jnp.float32)
    scores = jnp.einsum('rwthd,rwshd->rwhts', queries, key_vectors) * (1.0 / math.sqrt(head_depth)) + pair_bias[:, None]
    scores = jnp.where(allowed[:, None, None], scores, -1000000000.0)
    highest = lax.optimization_barrier(jnp.max(scores, axis=-1, keepdims=True))
    weights = jnp.exp(scores - highest)
    rounded = lax.optimization_barrier((weights / lax.optimization_barrier(jnp.sum(weights, axis=-1, keepdims=True))).astype(jnp.bfloat16))
    attention_weights = rounded.astype(jnp.float32)
    blended = jnp.einsum('rwhts,rwshd->rwthd', attention_weights, values).astype(jnp.bfloat16)
    blended = blended.reshape(window_rows, blocks, height, WLON, channels).transpose(0, 2, 1, 3, 4)
    return blended.reshape(window_rows, height, tile_span, channels)

def finish(inputs, attended, proj_weight, norm2_gain, fc1_weight, fc2_weight, recover_weight):
    resid = (inputs.astype(jnp.float32) + jnp.dot(attended, proj_weight, preferred_element_type=jnp.float32)).astype(jnp.bfloat16)
    normed2 = layer_norm(resid, norm2_gain).astype(jnp.bfloat16)
    hidden = jax.nn.gelu(jnp.dot(normed2, fc1_weight, preferred_element_type=jnp.float32), approximate=False).astype(jnp.bfloat16)
    block_out = (resid.astype(jnp.float32) + jnp.dot(hidden, fc2_weight, preferred_element_type=jnp.float32)).astype(jnp.bfloat16)
    patches = jnp.dot(block_out, recover_weight, preferred_element_type=jnp.float32).astype(jnp.bfloat16)
    lat_rows, lon_cols, pixel_channels = patches.shape
    variables = pixel_channels // 16
    shuffled = patches.reshape(lat_rows, lon_cols, variables, 4, 4).transpose(2, 0, 3, 1, 4)
    return shuffled.reshape(variables, lat_rows * 4, lon_cols * 4)

def reference(tokens, norm1_gain, qkv_weight, bias_table, bias_index, region_ids, proj_weight, norm2_gain, fc1_weight, fc2_weight, recover_weight, cotangent):

    def forward(inputs):
        projected = prepare(inputs, norm1_gain, qkv_weight)
        rolled = jnp.roll(projected, WLON // 2, axis=1)
        padded = jnp.pad(rolled, ((WLAT // 2, WLAT // 2), (0, 0), (0, 0)))
        grouped = padded.reshape(NWR, WLAT, LONG, 3 * C)
        edge_fill = jnp.full((WLAT // 2,), -1, jnp.int32)
        regions = jnp.concatenate([edge_fill, region_ids.astype(jnp.int32), edge_fill]).reshape(NWR, WLAT)

        def one_row(items):
            row_block, bias_row, index_row, region_row = items
            pair_bias = window_bias(bias_row[None], index_row[None])
            allowed = window_mask(region_row[None])
            return attend(row_block[None], pair_bias, allowed)[0]
        attended_rows = lax.map(one_row, (grouped, bias_table, bias_index, regions))
        attended = attended_rows.reshape(NWR * WLAT, LONG, C)[WLAT // 2:WLAT // 2 + LATG]
        attended = jnp.roll(attended, -(WLON // 2), axis=1)
        return finish(inputs, attended, proj_weight, norm2_gain, fc1_weight, fc2_weight, recover_weight)
    field, backward = jax.vjp(forward, tokens)
    token_grad = backward(cotangent)[0]
    return (field, token_grad)
```

```python
import functools
import math

import jax
import jax.numpy as jnp
from jax import lax
from jax.experimental import pallas as pl
from jax.experimental.pallas import tpu as pltpu
from jax.sharding import PartitionSpec as P

F32 = jnp.float32
BF16 = jnp.bfloat16
I32 = jnp.int32
MESH = pl.DeviceIdType.MESH

WLAT = 6
WLON = 12
SIDE = WLAT * WLON
HEADS = 6
DEPTH = 32
C = HEADS * DEPTH
MLP = 768
VARS = 5
ROWS = 6
COLS = 48
HALF = WLAT // 2
PAD = 16
WIDE = COLS + PAD
TALL = 2 * WLAT
SLOTS_PER_BAND = 2
BAND = SLOTS_PER_BAND * SIDE
TOKENS = 2 * BAND
LANES = 128
GROUP = 32
PIX = 4 * GROUP
EPS = 1e-05
LOG2E = math.log2(math.e)
SCALE = 1.0 / math.sqrt(DEPTH)
MASKED = -1.0e9
FRONT = LANES


def mm(a, b):
    return lax.dot_general(a, b, (((1,), (0,)), ((), ())), preferred_element_type=F32)


def mm_t(a, b):
    return lax.dot_general(a, b, (((1,), (1,)), ((), ())), preferred_element_type=F32)


def mm_tl(a, b):
    return lax.dot_general(a, b, (((0,), (0,)), ((), ())), preferred_element_type=F32)


def iota(shape, dim):
    return lax.broadcasted_iota(I32, shape, dim)


def one_hot(mask):
    return jnp.where(mask, 1.0, 0.0).astype(BF16)


def div12(t):
    return lax.shift_right_logical(t * 171, 11)


def div48(t):
    return jnp.where(t >= 144, 3, jnp.where(t >= 96, 2, jnp.where(t >= 48, 1, 0)))


def band_cells(t, upper, edge):
    slot = jnp.where(t >= SIDE, 1, 0)
    t = t - SIDE * slot
    i = div12(t)
    j = t - WLON * i
    left = (PAD - WLON // 2) + WLON * slot + j
    right = left + 2 * WLON
    if upper:
        usual = i * WIDE + left
        other = (i + HALF) * WIDE + right
        at_edge = jnp.logical_and(edge, i < HALF)
    else:
        usual = i * WIDE + right
        other = (i - HALF) * WIDE + left
        at_edge = jnp.logical_and(edge, i >= HALF)
    return jnp.where(at_edge, other, usual)


def mean_of(x):
    return jnp.sum(x, axis=-1, keepdims=True) * (1.0 / C)


def norm(x, gain):
    centered = x - mean_of(x)
    rstd = lax.rsqrt(mean_of(centered * centered) + EPS)
    xhat = centered * rstd
    return xhat, rstd, xhat * gain


def norm_back(d_out, xhat, rstd, gain):
    d_hat = d_out * gain
    return rstd * (d_hat - mean_of(d_hat) - xhat * mean_of(d_hat * xhat))


def gelu_parts(u):
    bell = jnp.exp2(u * u * (-0.5 * LOG2E))
    t = 1.0 / (1.0 + (0.3275911 * math.sqrt(0.5)) * jnp.abs(u))
    poly = t * (
        0.5 * 0.254829592
        + t
        * (
            0.5 * -0.284496736
            + t * (0.5 * 1.421413741 + t * (0.5 * -1.453152027 + t * (0.5 * 1.061405429)))
        )
    )
    tail = poly * bell
    cdf = jnp.where(u >= 0, 1.0 - tail, tail)
    return u * cdf, cdf + u * bell * (1.0 / math.sqrt(2.0 * math.pi))


def kernel(
    lats,
    lons,
    tok_hbm,
    g1_hbm,
    wqkv_hbm,
    table_hbm,
    index_hbm,
    region_hbm,
    wproj_hbm,
    g2_hbm,
    fc1_hbm,
    fc2_hbm,
    rec_hbm,
    cot_hbm,
    field_ref,
    grad_ref,
    ext_tok,
    ext_pix,
    back_pix,
    back_grad,
    got_pix_side,
    got_pix_low,
    got_pix_corner,
    got_pix_high,
    got_grad_side,
    got_grad_low,
    got_grad_corner,
    got_grad_high,
    g1_v,
    g2_v,
    wqkv,
    table,
    index,
    region,
    wproj,
    fc1,
    fc2,
    rec,
    cot,
    index_rows,
    index_square,
    bias,
    hidden_in,
    hidden,
    slope,
    weights_kept,
    local_sem,
    send_sem,
    recv_sem,
):
    lat = lax.axis_index("lat")
    lon = lax.axis_index("lon")
    first = lat == 0
    last = lat == lats - 1
    right = lax.rem(lon + 1, lons)
    left = lax.rem(lon + lons - 1, lons)
    above = lat - 1
    below = lat + 1

    barrier = pltpu.get_barrier_semaphore()

    def greet(row, column):
        pl.semaphore_signal(barrier, inc=1, device_id=(row, column), device_id_type=MESH)

    greet(lat, left)
    greet(lat, right)

    @pl.when(jnp.logical_not(first))
    def _():
        greet(above, lon)
        greet(above, left)

    @pl.when(jnp.logical_not(last))
    def _():
        greet(below, lon)
        greet(below, right)

    def local(src, dst, number):
        copy = pltpu.make_async_copy(src, dst, local_sem.at[number])
        copy.start()
        return copy

    cot_copy = local(cot_hbm, cot, 0)
    own_copy = local(tok_hbm, ext_tok.at[HALF : HALF + ROWS, PAD:WIDE], 1)
    index_copy = local(index_hbm, index, 2)
    table_copy = local(table_hbm.at[pl.ds(lat, 2)], table, 3)
    region_copy = local(region_hbm, region, 4)
    g1_copy = local(g1_hbm, g1_v, 5)
    wqkv_copy = local(wqkv_hbm, wqkv, 6)
    wproj_copy = local(wproj_hbm, wproj, 7)
    g2_copy = local(g2_hbm, g2_v, 8)
    fc1_copy = local(fc1_hbm, fc1, 9)
    fc2_copy = local(fc2_hbm, fc2, 10)
    rec_copy = local(rec_hbm, rec, 11)

    pl.semaphore_wait(barrier, 6 - 2 * jnp.where(first, 1, 0) - 2 * jnp.where(last, 1, 0))

    def remote(src, dst, number, row, column):
        return pltpu.make_async_remote_copy(
            src_ref=src,
            dst_ref=dst,
            send_sem=send_sem.at[number],
            recv_sem=recv_sem.at[number],
            device_id=(row, column),
            device_id_type=MESH,
        )

    def outward(src, ext, base):
        side = remote(
            src(slice(0, ROWS), slice(COLS - PAD, COLS)),
            ext.at[HALF : HALF + ROWS, 0:PAD],
            base,
            lat,
            right,
        )
        low = remote(
            src(slice(HALF, ROWS), slice(0, 2 * PAD)),
            ext.at[0:HALF, PAD : 3 * PAD],
            base + 1,
            below,
            lon,
        )
        corner = remote(
            src(slice(HALF, ROWS), slice(COLS - PAD, COLS)),
            ext.at[0:HALF, 0:PAD],
            base + 2,
            below,
            right,
        )
        high = remote(
            src(slice(0, HALF), slice(PAD, COLS)),
            ext.at[HALF + ROWS : TALL, 2 * PAD : WIDE],
            base + 3,
            above,
            lon,
        )
        return side, low, corner, high

    def homeward(ext, side_ref, low_ref, corner_ref, high_ref, base):
        side = remote(ext.at[HALF : HALF + ROWS, 0:PAD], side_ref, base, lat, left)
        low = remote(ext.at[0:HALF, PAD : 3 * PAD], low_ref, base + 1, above, lon)
        corner = remote(ext.at[0:HALF, 0:PAD], corner_ref, base + 2, above, left)
        high = remote(
            ext.at[HALF + ROWS : TALL, 2 * PAD : WIDE], high_ref, base + 3, below, lon
        )
        return side, low, corner, high

    def send(copies, down):
        side, low, corner, high = copies
        goes, comes = (last, first) if down else (first, last)
        side.start()

        @pl.when(jnp.logical_not(goes))
        def _():
            low.start()
            corner.start()

        @pl.when(jnp.logical_not(comes))
        def _():
            high.start()

    def receive(copies, down):
        side, low, corner, high = copies
        goes, comes = (last, first) if down else (first, last)
        side.wait_recv()

        @pl.when(jnp.logical_not(comes))
        def _():
            low.wait_recv()
            corner.wait_recv()

        @pl.when(jnp.logical_not(goes))
        def _():
            high.wait_recv()

    def sent(copies, down):
        side, low, corner, high = copies
        goes, comes = (last, first) if down else (first, last)
        side.wait_send()

        @pl.when(jnp.logical_not(goes))
        def _():
            low.wait_send()
            corner.wait_send()

        @pl.when(jnp.logical_not(comes))
        def _():
            high.wait_send()

    out_tok = outward(lambda a, b: tok_hbm.at[a, b], ext_tok, 0)
    send(out_tok, True)

    cot_copy.wait()
    r_col = iota((4 * COLS, 1), 0)
    j_col = div48(r_col)
    spread = one_hot(iota((4 * COLS, 4 * COLS), 1) == 4 * (r_col - COLS * j_col) + j_col)
    c_row = iota((1, ROWS * PIX), 1)
    a_row = lax.shift_right_logical(c_row, 7)
    vi_row = jnp.bitwise_and(c_row, GROUP - 1)
    v_row = lax.shift_right_logical(vi_row, 2)
    pix_row = jnp.where(
        vi_row < 4 * VARS, v_row * (4 * ROWS) + 4 * a_row + jnp.bitwise_and(vi_row, 3), -1
    )
    place = one_hot(iota((4 * VARS * ROWS, ROWS * PIX), 0) == pix_row)
    j_of_lane = jnp.bitwise_and(lax.shift_right_logical(c_row, 5), 3)

    pixels = cot[...].astype(F32).reshape(4 * VARS * ROWS, 4 * COLS).astype(BF16)
    by_column = mm_t(spread, pixels).astype(BF16)
    grouped = mm(by_column, place)
    by_token = jnp.zeros((COLS, ROWS * PIX), F32)
    for j in range(4):
        by_token = jnp.where(j_of_lane == j, grouped[j * COLS : (j + 1) * COLS], by_token)
    by_token = by_token.astype(BF16)
    for a in range(ROWS):
        ext_pix[HALF + a, PAD:WIDE, :] = by_token[:, a * PIX : (a + 1) * PIX]

    out_pix = outward(
        lambda a, b: ext_pix.at[
            slice(HALF + a.start, HALF + a.stop), slice(PAD + b.start, PAD + b.stop)
        ],
        ext_pix,
        4,
    )
    send(out_pix, True)

    for ext in (ext_tok, ext_pix):
        ext[0:HALF, 3 * PAD : WIDE] = jnp.zeros((HALF, PAD, ext.shape[2]), BF16)
        ext[HALF + ROWS : TALL, 0 : 2 * PAD] = jnp.zeros((HALF, 2 * PAD, ext.shape[2]), BF16)

        @pl.when(first)
        def _():
            ext[0:HALF, 0 : 3 * PAD] = jnp.zeros((HALF, 3 * PAD, ext.shape[2]), BF16)

        @pl.when(last)
        def _():
            ext[HALF + ROWS : TALL, 2 * PAD : WIDE] = jnp.zeros(
                (HALF, 2 * PAD, ext.shape[2]), BF16
            )

    index_copy.wait()
    index_rows[...] = jnp.zeros(index_rows.shape, I32)
    index_square[...] = jnp.zeros(index_square.shape, I32)
    pairs = SIDE * SIDE
    for band in range(2):
        index_rows[band : band + 1, FRONT : FRONT + pairs] = index[pl.ds(lat + band, 1), :]
    for t in range(SIDE):
        start = FRONT + SIDE * t
        usual = index_rows[:, start : start + SIDE]
        upper = usual[0:1]
        lower = usual[1:2]
        if t < SIDE // 2:
            start = FRONT + SIDE * (t + SIDE // 2) + SIDE // 2
            upper = jnp.where(first, index_rows[0:1, start : start + SIDE], upper)
        else:
            start = FRONT + SIDE * (t - SIDE // 2) - SIDE // 2
            lower = jnp.where(last, index_rows[1:2, start : start + SIDE], lower)
        index_square[0, t : t + 1, 0:SIDE] = upper
        index_square[1, t : t + 1, 0:SIDE] = lower

    table_copy.wait()
    region_copy.wait()
    k_col = iota((SIDE, 1), 0)
    q_row = iota((1, LANES), 1)
    i_col = div12(k_col)
    i_row = div12(q_row)
    slot_count = table.shape[2]
    for band in range(2):
        code_col = jnp.zeros((SIDE, 1), I32)
        code_row = jnp.zeros((1, LANES), I32)
        for i in range(WLAT):
            row = WLAT * lat - HALF + WLAT * band + i
            if band == 0 and i < HALF:
                row = row + jnp.where(first, HALF, 0)
            if band == 1 and i >= HALF:
                row = row - jnp.where(last, HALF, 0)
            code = region[row]
            if band == 0 and i < HALF:
                code = code + jnp.where(first, 1000, 0)
            if band == 1 and i < HALF:
                code = code + jnp.where(last, 1000, 0)
            code_col = jnp.where(i_col == i, code, code_col)
            code_row = jnp.where(i_row == i, code, code_row)
        allowed = code_col == code_row
        square = index_square[band].T[0:SIDE]
        lane = jnp.bitwise_and(square, LANES - 1)
        chunk = lax.shift_right_logical(square, 7)
        for h in range(HEADS):
            picked = jnp.zeros((SIDE, LANES), F32)
            for c in range(-(-slot_count // LANES)):
                stop = min(slot_count, (c + 1) * LANES)
                part = table[band, h : h + 1, c * LANES : stop]
                if stop - c * LANES < LANES:
                    part = jnp.concatenate(
                        [part, jnp.zeros((1, LANES - (stop - c * LANES)), F32)], axis=1
                    )
                found = jnp.take_along_axis(
                    jnp.broadcast_to(part, (SIDE, LANES)), lane, axis=1, mode="promise_in_bounds"
                )
                picked = jnp.where(chunk == c, found, picked)
            bias[band, h] = jnp.where(allowed, picked * LOG2E, MASKED)[:, 0:SIDE]

    chosen = []
    chosen_t = []
    for band in range(2):
        edge = first if band == 0 else last
        cells = band_cells(iota((BAND, 1), 0), band == 0, edge)
        chosen.append(one_hot(iota((BAND, WLAT * WIDE), 1) == cells))
        cells = band_cells(iota((1, BAND), 1), band == 0, edge)
        chosen_t.append(one_hot(iota((WLAT * WIDE, BAND), 0) == cells))

    def to_windows(ext):
        width = ext.shape[2]
        return jnp.concatenate(
            [
                mm(
                    chosen[band],
                    ext[band * WLAT : (band + 1) * WLAT].reshape(WLAT * WIDE, width),
                )
                for band in range(2)
            ],
            axis=0,
        )

    def to_grid(values, ext):
        width = ext.shape[2]
        for band in range(2):
            ext[band * WLAT : (band + 1) * WLAT] = (
                mm(chosen_t[band], values[band * BAND : (band + 1) * BAND])
                .astype(BF16)
                .reshape(WLAT, WIDE, width)
            )

    g1_copy.wait()
    g2_copy.wait()
    wqkv_copy.wait()
    wproj_copy.wait()
    fc1_copy.wait()
    fc2_copy.wait()
    rec_copy.wait()
    own_copy.wait()
    gain1 = g1_v[...].reshape(1, C)
    gain2 = g2_v[...].reshape(1, C)

    c_lane = iota((1, PIX), 1)
    vi_lane = jnp.bitwise_and(c_lane, GROUP - 1)
    source = (
        16 * lax.shift_right_logical(vi_lane, 2)
        + 4 * jnp.bitwise_and(vi_lane, 3)
        + lax.shift_right_logical(c_lane, 5)
    )
    source = jnp.where(vi_lane < 4 * VARS, source, -1)
    rec_wide = mm(rec[...], one_hot(iota((16 * VARS, PIX), 0) == source)).astype(BF16)

    head_of_lane = lax.shift_right_logical(iota((HEADS, 1, C), 2), 5)
    head_mask = jnp.where(head_of_lane == iota((HEADS, 1, C), 0), 1.0, 0.0)

    receive(out_tok, True)
    tokens = to_windows(ext_tok)

    xhat1, rstd1, normed = norm(tokens, gain1)
    normed = normed.astype(BF16)
    wq = wqkv[:, 0:C]
    wk = wqkv[:, C : 2 * C]
    wv = wqkv[:, 2 * C : 3 * C]
    query = mm(normed, wq).astype(BF16).astype(F32)
    key = mm(normed, wk).astype(BF16).astype(F32)
    value = mm(normed, wv).astype(BF16).astype(F32)

    def stack(x):
        return (x[None] * head_mask).reshape(HEADS * SIDE, C).astype(BF16)

    def by_head(x):
        return jnp.sum(x.reshape(HEADS, SIDE, C) * head_mask, axis=0)

    key_stacks = []
    value_stacks = []
    attended = []
    for slot in range(4):
        rows = slice(slot * SIDE, (slot + 1) * SIDE)
        key_stack = stack(key[rows])
        value_stack = stack(value[rows])
        key_stacks.append(key_stack)
        value_stacks.append(value_stack)
        scores = mm_t(key_stack, query[rows].astype(BF16))
        parts = []
        for h in range(HEADS):
            s = scores[h * SIDE : (h + 1) * SIDE] * (SCALE * LOG2E) + bias[slot // 2, h]
            s = jnp.exp2(s - jnp.max(s, axis=0, keepdims=True))
            p = s * (1.0 / jnp.sum(s, axis=0, keepdims=True))
            weights_kept[slot, h] = p
            parts.append(p)
        weights = jnp.concatenate(parts, axis=0).astype(BF16)
        attended.append(mm_tl(weights, value_stack))
    attended = jnp.concatenate(attended, axis=0).astype(BF16)

    resid = (tokens + mm(attended, wproj[...])).astype(BF16)
    xhat2, rstd2, normed2 = norm(resid.astype(F32), gain2)
    hidden_in[...] = mm(normed2.astype(BF16), fc1[...])

    def gelu_rows(n, _):
        rows = pl.ds(pl.multiple_of(n * 16, 16), 16)
        out, derivative = gelu_parts(hidden_in[rows, :])
        hidden[rows, :] = out.astype(BF16)
        slope[rows, :] = derivative
        return 0

    lax.fori_loop(0, TOKENS // 16, gelu_rows, 0)
    block_out = (resid.astype(F32) + mm(hidden[...], fc2[...])).astype(BF16)
    to_grid(mm(block_out, rec_wide).astype(BF16), back_pix)
    home_pix = homeward(
        back_pix, got_pix_side, got_pix_low, got_pix_corner, got_pix_high, 8
    )
    send(home_pix, False)

    receive(out_pix, True)
    d_block = mm_t(to_windows(ext_pix).astype(BF16), rec_wide).astype(BF16)
    hidden_in[...] = mm_t(d_block, fc2[...])

    def gelu_back_rows(n, _):
        rows = pl.ds(pl.multiple_of(n * 16, 16), 16)
        d_hidden = hidden_in[rows, :].astype(BF16).astype(F32)
        hidden[rows, :] = (d_hidden * slope[rows, :]).astype(BF16)
        return 0

    lax.fori_loop(0, TOKENS // 16, gelu_back_rows, 0)
    d_normed2 = mm_t(hidden[...], fc1[...]).astype(BF16).astype(F32)
    d_resid = (
        d_block.astype(F32) + norm_back(d_normed2, xhat2, rstd2, gain2).astype(BF16).astype(F32)
    ).astype(BF16)
    d_attended = mm_t(d_resid, wproj[...]).astype(BF16).astype(F32)

    d_query = []
    d_key = []
    d_value = []
    for slot in range(4):
        rows = slice(slot * SIDE, (slot + 1) * SIDE)
        d_out = d_attended[rows].astype(BF16)
        d_weights = mm_t(value_stacks[slot], d_out)
        parts = []
        weights = []
        for h in range(HEADS):
            p = weights_kept[slot, h]
            d = d_weights[h * SIDE : (h + 1) * SIDE]
            pd = p * d
            parts.append((pd - p * jnp.sum(pd, axis=0, keepdims=True)) * SCALE)
            weights.append(p)
        d_scores = jnp.concatenate(parts, axis=0).astype(BF16)
        weights = jnp.concatenate(weights, axis=0).astype(BF16)
        d_value.append(by_head(mm(weights, d_out)))
        d_query.append(mm_tl(d_scores, key_stacks[slot]))
        d_key.append(by_head(mm(d_scores, query[rows].astype(BF16))))
    d_query = jnp.concatenate(d_query, axis=0).astype(BF16)
    d_key = jnp.concatenate(d_key, axis=0).astype(BF16)
    d_value = jnp.concatenate(d_value, axis=0).astype(BF16)

    d_normed = mm_t(d_query, wq) + mm_t(d_key, wk) + mm_t(d_value, wv)
    d_normed = d_normed.astype(BF16).astype(F32)
    through = norm_back(d_normed, xhat1, rstd1, gain1).astype(BF16).astype(F32)
    to_grid((d_resid.astype(F32) + through).astype(BF16), back_grad)
    home_grad = homeward(
        back_grad, got_grad_side, got_grad_low, got_grad_corner, got_grad_high, 12
    )
    send(home_grad, False)

    def gather_home(ext, side, low, corner, high):
        width = ext.shape[2]
        own = ext[HALF : HALF + ROWS, PAD:WIDE, :].astype(F32)
        from_side = side[...].astype(F32)
        from_low = jnp.where(last, 0.0, low[...].astype(F32))
        from_corner = jnp.where(last, 0.0, corner[...].astype(F32))
        from_high = jnp.where(first, 0.0, high[...].astype(F32))
        upper = jnp.concatenate(
            [
                own[0:HALF, 0:PAD],
                own[0:HALF, PAD : 2 * PAD] + from_high[:, 0:PAD],
                own[0:HALF, 2 * PAD :] + from_high[:, PAD:] + from_side[0:HALF],
            ],
            axis=1,
        )
        lower = jnp.concatenate(
            [
                own[HALF:, 0 : 2 * PAD] + from_low,
                own[HALF:, 2 * PAD :] + from_corner + from_side[HALF:],
            ],
            axis=1,
        )
        return jnp.concatenate([upper, lower], axis=0)

    receive(home_pix, False)
    patches = gather_home(
        back_pix, got_pix_side, got_pix_low, got_pix_corner, got_pix_high
    )
    patches = jnp.concatenate([patches[a] for a in range(ROWS)], axis=1)
    patches = jnp.concatenate(
        [jnp.where(j_of_lane == j, patches, 0.0) for j in range(4)], axis=0
    ).astype(BF16)
    by_pixel = mm_t(place, patches).astype(BF16)
    field = mm(by_pixel, spread)
    field_ref[...] = field.reshape(VARS, 4 * ROWS, 4 * COLS).astype(BF16)

    receive(home_grad, False)
    grad_ref[...] = gather_home(
        back_grad, got_grad_side, got_grad_low, got_grad_corner, got_grad_high
    ).astype(BF16)

    sent(out_tok, True)
    sent(out_pix, True)
    sent(home_pix, False)
    sent(home_grad, False)


def per_device(lats, lons, *args):
    tokens, _, _, table, index, region = args[:6]
    cot = args[-1]
    scratch = [
        pltpu.VMEM((TALL, WIDE, C), BF16),
        pltpu.VMEM((TALL, WIDE, PIX), BF16),
        pltpu.VMEM((TALL, WIDE, PIX), BF16),
        pltpu.VMEM((TALL, WIDE, C), BF16),
    ]
    for width in (PIX, C):
        scratch += [
            pltpu.VMEM((ROWS, PAD, width), BF16),
            pltpu.VMEM((HALF, 2 * PAD, width), BF16),
            pltpu.VMEM((HALF, PAD, width), BF16),
            pltpu.VMEM((HALF, 2 * PAD, width), BF16),
        ]
    scratch += [
        pltpu.VMEM((C,), F32),
        pltpu.VMEM((C,), F32),
        pltpu.VMEM((C, 3 * C), BF16),
        pltpu.VMEM((2,) + table.shape[1:], F32),
        pltpu.VMEM(index.shape, I32),
        pltpu.SMEM(region.shape, I32),
        pltpu.VMEM((C, C), BF16),
        pltpu.VMEM((C, MLP), BF16),
        pltpu.VMEM((MLP, C), BF16),
        pltpu.VMEM((C, 16 * VARS), BF16),
        pltpu.VMEM(cot.shape, BF16),
        pltpu.VMEM((2, FRONT + 41 * LANES + LANES), I32),
        pltpu.VMEM((2, LANES, LANES), I32),
        pltpu.VMEM((2, HEADS, SIDE, SIDE), F32),
        pltpu.VMEM((TOKENS, MLP), F32),
        pltpu.VMEM((TOKENS, MLP), BF16),
        pltpu.VMEM((TOKENS, MLP), F32),
        pltpu.VMEM((4, HEADS, SIDE, SIDE), F32),
        pltpu.SemaphoreType.DMA((12,)),
        pltpu.SemaphoreType.DMA((16,)),
        pltpu.SemaphoreType.DMA((16,)),
    ]
    return pl.pallas_call(
        functools.partial(kernel, lats, lons),
        out_shape=(
            jax.ShapeDtypeStruct(cot.shape, BF16),
            jax.ShapeDtypeStruct(tokens.shape, BF16),
        ),
        in_specs=[pl.BlockSpec(memory_space=pl.ANY)] * 12,
        out_specs=(
            pl.BlockSpec(memory_space=pltpu.VMEM),
            pl.BlockSpec(memory_space=pltpu.VMEM),
        ),
        scratch_shapes=scratch,
        compiler_params=pltpu.CompilerParams(
            collective_id=0, has_side_effects=True, vmem_limit_bytes=40 * 1024 * 1024
        ),
    )(*args)


def solution(mesh):
    return jax.shard_map(
        functools.partial(per_device, mesh.shape["lat"], mesh.shape["lon"]),
        mesh=mesh,
        in_specs=(P("lat", "lon", None),) + (P(),) * 10 + (P(None, "lat", "lon"),),
        out_specs=(P(None, "lat", "lon"), P("lat", "lon", None)),
        check_vma=False,
    )
```

```python
import functools
import math

import jax
import jax.numpy as jnp
from jax import lax
from jax.experimental import pallas as pl
from jax.experimental.pallas import tpu as pltpu
from jax.sharding import PartitionSpec as P

F32 = jnp.float32
BF16 = jnp.bfloat16
I32 = jnp.int32
MESH = pl.DeviceIdType.MESH

WLAT = 6
WLON = 12
SIDE = WLAT * WLON
HEADS = 6
DEPTH = 32
C = HEADS * DEPTH
MLP = 768
VARS = 5
ROWS = 6
COLS = 48
HALF = WLAT // 2
PAD = 16
WIDE = COLS + PAD
TALL = 2 * WLAT
SLOTS_PER_BAND = 2
BAND = SLOTS_PER_BAND * SIDE
TOKENS = 2 * BAND
LANES = 128
GROUP = 32
PIX = 4 * GROUP
EPS = 1e-05
LOG2E = math.log2(math.e)
SCALE = 1.0 / math.sqrt(DEPTH)
MASKED = -1.0e9
FRONT = LANES


def mm(a, b):
    return lax.dot_general(a, b, (((1,), (0,)), ((), ())), preferred_element_type=F32)


def mm_t(a, b):
    return lax.dot_general(a, b, (((1,), (1,)), ((), ())), preferred_element_type=F32)


def mm_tl(a, b):
    return lax.dot_general(a, b, (((0,), (0,)), ((), ())), preferred_element_type=F32)


def iota(shape, dim):
    return lax.broadcasted_iota(I32, shape, dim)


def one_hot(mask):
    return jnp.where(mask, 1.0, 0.0).astype(BF16)


def div12(t):
    return lax.shift_right_logical(t * 171, 11)


def div48(t):
    return jnp.where(t >= 144, 3, jnp.where(t >= 96, 2, jnp.where(t >= 48, 1, 0)))


def band_cells(t, upper, edge):
    slot = jnp.where(t >= SIDE, 1, 0)
    t = t - SIDE * slot
    i = div12(t)
    j = t - WLON * i
    left = (PAD - WLON // 2) + WLON * slot + j
    right = left + 2 * WLON
    if upper:
        usual = i * WIDE + left
        other = (i + HALF) * WIDE + right
        at_edge = jnp.logical_and(edge, i < HALF)
    else:
        usual = i * WIDE + right
        other = (i - HALF) * WIDE + left
        at_edge = jnp.logical_and(edge, i >= HALF)
    return jnp.where(at_edge, other, usual)


def mean_of(x):
    return jnp.sum(x, axis=-1, keepdims=True) * (1.0 / C)


def norm(x, gain):
    centered = x - mean_of(x)
    rstd = lax.rsqrt(mean_of(centered * centered) + EPS)
    xhat = centered * rstd
    return xhat, rstd, xhat * gain


def norm_back(d_out, xhat, rstd, gain):
    d_hat = d_out * gain
    return rstd * (d_hat - mean_of(d_hat) - xhat * mean_of(d_hat * xhat))


def gelu_parts(u):
    bell = jnp.exp2(u * u * (-0.5 * LOG2E))
    t = 1.0 / (1.0 + (0.3275911 * math.sqrt(0.5)) * jnp.abs(u))
    poly = t * (
        0.5 * 0.254829592
        + t
        * (
            0.5 * -0.284496736
            + t * (0.5 * 1.421413741 + t * (0.5 * -1.453152027 + t * (0.5 * 1.061405429)))
        )
    )
    tail = poly * bell
    cdf = jnp.where(u >= 0, 1.0 - tail, tail)
    return u * cdf, cdf + u * bell * (1.0 / math.sqrt(2.0 * math.pi))


def kernel(
    lats,
    lons,
    tok_hbm,
    g1_hbm,
    wqkv_hbm,
    table_hbm,
    index_hbm,
    region_hbm,
    wproj_hbm,
    g2_hbm,
    fc1_hbm,
    fc2_hbm,
    rec_hbm,
    cot_hbm,
    field_ref,
    grad_ref,
    ext_tok,
    ext_pix,
    back_pix,
    back_grad,
    got_pix_side,
    got_pix_low,
    got_pix_corner,
    got_pix_high,
    got_grad_side,
    got_grad_low,
    got_grad_corner,
    got_grad_high,
    g1_v,
    g2_v,
    wqkv,
    table,
    index,
    region,
    wproj,
    fc1,
    fc2,
    rec,
    cot,
    index_rows,
    index_square,
    bias,
    hidden_in,
    hidden,
    slope,
    weights_kept,
    local_sem,
    send_sem,
    recv_sem,
):
    lat = lax.axis_index("lat")
    lon = lax.axis_index("lon")
    first = lat == 0
    last = lat == lats - 1
    right = lax.rem(lon + 1, lons)
    left = lax.rem(lon + lons - 1, lons)
    above = lat - 1
    below = lat + 1

    barrier = pltpu.get_barrier_semaphore()

    def greet(row, column):
        pl.semaphore_signal(barrier, inc=1, device_id=(row, column), device_id_type=MESH)

    greet(lat, left)
    greet(lat, right)

    @pl.when(jnp.logical_not(first))
    def _():
        greet(above, lon)
        greet(above, left)

    @pl.when(jnp.logical_not(last))
    def _():
        greet(below, lon)
        greet(below, right)

    def local(src, dst, number):
        copy = pltpu.make_async_copy(src, dst, local_sem.at[number])
        copy.start()
        return copy

    cot_copy = local(cot_hbm, cot, 0)
    own_copy = local(tok_hbm, ext_tok.at[HALF : HALF + ROWS, PAD:WIDE], 1)
    index_copy = local(index_hbm, index, 2)
    table_copy = local(table_hbm.at[pl.ds(lat, 2)], table, 3)
    region_copy = local(region_hbm, region, 4)
    g1_copy = local(g1_hbm, g1_v, 5)
    wqkv_copy = local(wqkv_hbm, wqkv, 6)
    wproj_copy = local(wproj_hbm, wproj, 7)
    g2_copy = local(g2_hbm, g2_v, 8)
    fc1_copy = local(fc1_hbm, fc1, 9)
    fc2_copy = local(fc2_hbm, fc2, 10)
    rec_copy = local(rec_hbm, rec, 11)

    pl.semaphore_wait(barrier, 6 - 2 * jnp.where(first, 1, 0) - 2 * jnp.where(last, 1, 0))

    def remote(src, dst, number, row, column):
        return pltpu.make_async_remote_copy(
            src_ref=src,
            dst_ref=dst,
            send_sem=send_sem.at[number],
            recv_sem=recv_sem.at[number],
            device_id=(row, column),
            device_id_type=MESH,
        )

    def outward(src, ext, base):
        side = remote(
            src(slice(0, ROWS), slice(COLS - PAD, COLS)),
            ext.at[HALF : HALF + ROWS, 0:PAD],
            base,
            lat,
            right,
        )
        low = remote(
            src(slice(HALF, ROWS), slice(0, 2 * PAD)),
            ext.at[0:HALF, PAD : 3 * PAD],
            base + 1,
            below,
            lon,
        )
        corner = remote(
            src(slice(HALF, ROWS), slice(COLS - PAD, COLS)),
            ext.at[0:HALF, 0:PAD],
            base + 2,
            below,
            right,
        )
        high = remote(
            src(slice(0, HALF), slice(PAD, COLS)),
            ext.at[HALF + ROWS : TALL, 2 * PAD : WIDE],
            base + 3,
            above,
            lon,
        )
        return side, low, corner, high

    def homeward(ext, side_ref, low_ref, corner_ref, high_ref, base):
        side = remote(ext.at[HALF : HALF + ROWS, 0:PAD], side_ref, base, lat, left)
        low = remote(ext.at[0:HALF, PAD : 3 * PAD], low_ref, base + 1, above, lon)
        corner = remote(ext.at[0:HALF, 0:PAD], corner_ref, base + 2, above, left)
        high = remote(
            ext.at[HALF + ROWS : TALL, 2 * PAD : WIDE], high_ref, base + 3, below, lon
        )
        return side, low, corner, high

    def send(copies, down):
        side, low, corner, high = copies
        goes, comes = (last, first) if down else (first, last)
        side.start()

        @pl.when(jnp.logical_not(goes))
        def _():
            low.start()
            corner.start()

        @pl.when(jnp.logical_not(comes))
        def _():
            high.start()

    def receive(copies, down):
        side, low, corner, high = copies
        goes, comes = (last, first) if down else (first, last)
        side.wait_recv()

        @pl.when(jnp.logical_not(comes))
        def _():
            low.wait_recv()
            corner.wait_recv()

        @pl.when(jnp.logical_not(goes))
        def _():
            high.wait_recv()

    def sent(copies, down):
        side, low, corner, high = copies
        goes, comes = (last, first) if down else (first, last)
        side.wait_send()

        @pl.when(jnp.logical_not(goes))
        def _():
            low.wait_send()
            corner.wait_send()

        @pl.when(jnp.logical_not(comes))
        def _():
            high.wait_send()

    out_tok = outward(lambda a, b: tok_hbm.at[a, b], ext_tok, 0)
    send(out_tok, True)

    cot_copy.wait()
    r_col = iota((4 * COLS, 1), 0)
    j_col = div48(r_col)
    spread = one_hot(iota((4 * COLS, 4 * COLS), 1) == 4 * (r_col - COLS * j_col) + j_col)
    c_row = iota((1, ROWS * PIX), 1)
    a_row = lax.shift_right_logical(c_row, 7)
    vi_row = jnp.bitwise_and(c_row, GROUP - 1)
    v_row = lax.shift_right_logical(vi_row, 2)
    pix_row = jnp.where(
        vi_row < 4 * VARS, v_row * (4 * ROWS) + 4 * a_row + jnp.bitwise_and(vi_row, 3), -1
    )
    place = one_hot(iota((4 * VARS * ROWS, ROWS * PIX), 0) == pix_row)
    j_of_lane = jnp.bitwise_and(lax.shift_right_logical(c_row, 5), 3)

    pixels = cot[...].astype(F32).reshape(4 * VARS * ROWS, 4 * COLS).astype(BF16)
    by_column = mm_t(spread, pixels).astype(BF16)
    grouped = mm(by_column, place)
    by_token = jnp.zeros((COLS, ROWS * PIX), F32)
    for j in range(4):
        by_token = jnp.where(j_of_lane == j, grouped[j * COLS : (j + 1) * COLS], by_token)
    by_token = by_token.astype(BF16)
    for a in range(ROWS):
        ext_pix[HALF + a, PAD:WIDE, :] = by_token[:, a * PIX : (a + 1) * PIX]

    out_pix = outward(
        lambda a, b: ext_pix.at[
            slice(HALF + a.start, HALF + a.stop), slice(PAD + b.start, PAD + b.stop)
        ],
        ext_pix,
        4,
    )
    send(out_pix, True)

    for ext in (ext_tok, ext_pix):
        ext[0:HALF, 3 * PAD : WIDE] = jnp.zeros((HALF, PAD, ext.shape[2]), BF16)
        ext[HALF + ROWS : TALL, 0 : 2 * PAD] = jnp.zeros((HALF, 2 * PAD, ext.shape[2]), BF16)

        @pl.when(first)
        def _():
            ext[0:HALF, 0 : 3 * PAD] = jnp.zeros((HALF, 3 * PAD, ext.shape[2]), BF16)

        @pl.when(last)
        def _():
            ext[HALF + ROWS : TALL, 2 * PAD : WIDE] = jnp.zeros(
                (HALF, 2 * PAD, ext.shape[2]), BF16
            )

    index_copy.wait()
    index_rows[...] = jnp.zeros(index_rows.shape, I32)
    index_square[...] = jnp.zeros(index_square.shape, I32)
    pairs = SIDE * SIDE
    for band in range(2):
        index_rows[band : band + 1, FRONT : FRONT + pairs] = index[pl.ds(lat + band, 1), :]
    for t in range(SIDE):
        start = FRONT + SIDE * t
        usual = index_rows[:, start : start + SIDE]
        upper = usual[0:1]
        lower = usual[1:2]
        if t < SIDE // 2:
            start = FRONT + SIDE * (t + SIDE // 2) + SIDE // 2
            upper = jnp.where(first, index_rows[0:1, start : start + SIDE], upper)
        else:
            start = FRONT + SIDE * (t - SIDE // 2) - SIDE // 2
            lower = jnp.where(last, index_rows[1:2, start : start + SIDE], lower)
        index_square[0, t : t + 1, 0:SIDE] = upper
        index_square[1, t : t + 1, 0:SIDE] = lower

    table_copy.wait()
    region_copy.wait()
    k_col = iota((SIDE, 1), 0)
    q_row = iota((1, LANES), 1)
    i_col = div12(k_col)
    i_row = div12(q_row)
    slot_count = table.shape[2]
    for band in range(2):
        code_col = jnp.zeros((SIDE, 1), I32)
        code_row = jnp.zeros((1, LANES), I32)
        for i in range(WLAT):
            row = WLAT * lat - HALF + WLAT * band + i
            if band == 0 and i < HALF:
                row = row + jnp.where(first, HALF, 0)
            if band == 1 and i >= HALF:
                row = row - jnp.where(last, HALF, 0)
            code = region[row]
            if band == 0 and i < HALF:
                code = code + jnp.where(first, 1000, 0)
            if band == 1 and i < HALF:
                code = code + jnp.where(last, 1000, 0)
            code_col = jnp.where(i_col == i, code, code_col)
            code_row = jnp.where(i_row == i, code, code_row)
        allowed = code_col == code_row
        square = index_square[band].T[0:SIDE]
        lane = jnp.bitwise_and(square, LANES - 1)
        chunk = lax.shift_right_logical(square, 7)
        for h in range(HEADS):
            picked = jnp.zeros((SIDE, LANES), F32)
            for c in range(-(-slot_count // LANES)):
                stop = min(slot_count, (c + 1) * LANES)
                part = table[band, h : h + 1, c * LANES : stop]
                if stop - c * LANES < LANES:
                    part = jnp.concatenate(
                        [part, jnp.zeros((1, LANES - (stop - c * LANES)), F32)], axis=1
                    )
                found = jnp.take_along_axis(
                    jnp.broadcast_to(part, (SIDE, LANES)), lane, axis=1, mode="promise_in_bounds"
                )
                picked = jnp.where(chunk == c, found, picked)
            bias[band, h] = jnp.where(allowed, picked * LOG2E, MASKED)[:, 0:SIDE]

    chosen = []
    chosen_t = []
    for band in range(2):
        edge = first if band == 0 else last
        cells = band_cells(iota((BAND, 1), 0), band == 0, edge)
        chosen.append(one_hot(iota((BAND, WLAT * WIDE), 1) == cells))
        cells = band_cells(iota((1, BAND), 1), band == 0, edge)
        chosen_t.append(one_hot(iota((WLAT * WIDE, BAND), 0) == cells))

    def to_windows(ext):
        width = ext.shape[2]
        return jnp.concatenate(
            [
                mm(
                    chosen[band],
                    ext[band * WLAT : (band + 1) * WLAT].reshape(WLAT * WIDE, width),
                )
                for band in range(2)
            ],
            axis=0,
        )

    def to_grid(values, ext):
        width = ext.shape[2]
        for band in range(2):
            ext[band * WLAT : (band + 1) * WLAT] = (
                mm(chosen_t[band], values[band * BAND : (band + 1) * BAND])
                .astype(BF16)
                .reshape(WLAT, WIDE, width)
            )

    g1_copy.wait()
    g2_copy.wait()
    wqkv_copy.wait()
    wproj_copy.wait()
    fc1_copy.wait()
    fc2_copy.wait()
    rec_copy.wait()
    own_copy.wait()
    gain1 = g1_v[...].reshape(1, C)
    gain2 = g2_v[...].reshape(1, C)

    c_lane = iota((PIX, 1), 0)
    vi_lane = jnp.bitwise_and(c_lane, GROUP - 1)
    source = (
        16 * lax.shift_right_logical(vi_lane, 2)
        + 4 * jnp.bitwise_and(vi_lane, 3)
        + lax.shift_right_logical(c_lane, 5)
    )
    source = jnp.where(vi_lane < 4 * VARS, source, -1)
    source = one_hot(iota((PIX, 16 * VARS), 1) == source)
    rec_wide = mm(source, rec[...]).astype(BF16)

    head_of_lane = lax.shift_right_logical(iota((HEADS, 1, C), 2), 5)
    head_mask = jnp.where(head_of_lane == iota((HEADS, 1, C), 0), 1.0, 0.0)

    receive(out_tok, True)
    tokens = to_windows(ext_tok)

    xhat1, rstd1, normed = norm(tokens, gain1)
    normed = normed.astype(BF16)
    wq = wqkv[:, 0:C]
    wk = wqkv[:, C : 2 * C]
    wv = wqkv[:, 2 * C : 3 * C]
    query = mm(normed, wq).astype(BF16).astype(F32)
    key = mm(normed, wk).astype(BF16).astype(F32)
    value = mm(normed, wv).astype(BF16).astype(F32)

    def stack(x):
        return (x[None] * head_mask).reshape(HEADS * SIDE, C).astype(BF16)

    def by_head(x):
        return jnp.sum(x.reshape(HEADS, SIDE, C) * head_mask, axis=0)

    key_stacks = []
    value_stacks = []
    attended = []
    for slot in range(4):
        rows = slice(slot * SIDE, (slot + 1) * SIDE)
        key_stack = stack(key[rows])
        value_stack = stack(value[rows])
        key_stacks.append(key_stack)
        value_stacks.append(value_stack)
        scores = mm_t(key_stack, query[rows].astype(BF16))
        parts = []
        for h in range(HEADS):
            s = scores[h * SIDE : (h + 1) * SIDE] * (SCALE * LOG2E) + bias[slot // 2, h]
            s = jnp.exp2(s - jnp.max(s, axis=0, keepdims=True))
            p = s * (1.0 / jnp.sum(s, axis=0, keepdims=True))
            weights_kept[slot, h] = p
            parts.append(p)
        weights = jnp.concatenate(parts, axis=0).astype(BF16)
        attended.append(mm_tl(weights, value_stack))
    attended = jnp.concatenate(attended, axis=0).astype(BF16)

    resid = (tokens + mm(attended, wproj[...])).astype(BF16)
    xhat2, rstd2, normed2 = norm(resid.astype(F32), gain2)
    hidden_in[...] = mm(normed2.astype(BF16), fc1[...])

    def gelu_rows(n, _):
        rows = pl.ds(pl.multiple_of(n * 16, 16), 16)
        out, derivative = gelu_parts(hidden_in[rows, :])
        hidden[rows, :] = out.astype(BF16)
        slope[rows, :] = derivative
        return 0

    lax.fori_loop(0, TOKENS // 16, gelu_rows, 0)
    block_out = (resid.astype(F32) + mm_t(hidden[...], fc2[...])).astype(BF16)
    to_grid(mm_t(block_out, rec_wide).astype(BF16), back_pix)
    home_pix = homeward(
        back_pix, got_pix_side, got_pix_low, got_pix_corner, got_pix_high, 8
    )
    send(home_pix, False)

    receive(out_pix, True)
    d_block = mm(to_windows(ext_pix).astype(BF16), rec_wide).astype(BF16)
    hidden_in[...] = mm(d_block, fc2[...])

    def gelu_back_rows(n, _):
        rows = pl.ds(pl.multiple_of(n * 16, 16), 16)
        d_hidden = hidden_in[rows, :].astype(BF16).astype(F32)
        hidden[rows, :] = (d_hidden * slope[rows, :]).astype(BF16)
        return 0

    lax.fori_loop(0, TOKENS // 16, gelu_back_rows, 0)
    d_normed2 = mm_t(hidden[...], fc1[...]).astype(BF16).astype(F32)
    d_resid = (
        d_block.astype(F32) + norm_back(d_normed2, xhat2, rstd2, gain2).astype(BF16).astype(F32)
    ).astype(BF16)
    d_attended = mm_t(d_resid, wproj[...]).astype(BF16).astype(F32)

    d_query = []
    d_key = []
    d_value = []
    for slot in range(4):
        rows = slice(slot * SIDE, (slot + 1) * SIDE)
        d_out = d_attended[rows].astype(BF16)
        d_weights = mm_t(value_stacks[slot], d_out)
        parts = []
        weights = []
        for h in range(HEADS):
            p = weights_kept[slot, h]
            d = d_weights[h * SIDE : (h + 1) * SIDE]
            pd = p * d
            parts.append((pd - p * jnp.sum(pd, axis=0, keepdims=True)) * SCALE)
            weights.append(p)
        d_scores = jnp.concatenate(parts, axis=0).astype(BF16)
        weights = jnp.concatenate(weights, axis=0).astype(BF16)
        d_value.append(by_head(mm(weights, d_out)))
        d_query.append(mm_tl(d_scores, key_stacks[slot]))
        d_key.append(by_head(mm(d_scores, query[rows].astype(BF16))))
    d_query = jnp.concatenate(d_query, axis=0).astype(BF16)
    d_key = jnp.concatenate(d_key, axis=0).astype(BF16)
    d_value = jnp.concatenate(d_value, axis=0).astype(BF16)

    d_normed = mm_t(d_query, wq) + mm_t(d_key, wk) + mm_t(d_value, wv)
    d_normed = d_normed.astype(BF16).astype(F32)
    through = norm_back(d_normed, xhat1, rstd1, gain1).astype(BF16).astype(F32)
    to_grid((d_resid.astype(F32) + through).astype(BF16), back_grad)
    home_grad = homeward(
        back_grad, got_grad_side, got_grad_low, got_grad_corner, got_grad_high, 12
    )
    send(home_grad, False)

    def gather_home(ext, side, low, corner, high):
        width = ext.shape[2]
        own = ext[HALF : HALF + ROWS, PAD:WIDE, :].astype(F32)
        from_side = side[...].astype(F32)
        from_low = jnp.where(last, 0.0, low[...].astype(F32))
        from_corner = jnp.where(last, 0.0, corner[...].astype(F32))
        from_high = jnp.where(first, 0.0, high[...].astype(F32))
        upper = jnp.concatenate(
            [
                own[0:HALF, 0:PAD],
                own[0:HALF, PAD : 2 * PAD] + from_high[:, 0:PAD],
                own[0:HALF, 2 * PAD :] + from_high[:, PAD:] + from_side[0:HALF],
            ],
            axis=1,
        )
        lower = jnp.concatenate(
            [
                own[HALF:, 0 : 2 * PAD] + from_low,
                own[HALF:, 2 * PAD :] + from_corner + from_side[HALF:],
            ],
            axis=1,
        )
        return jnp.concatenate([upper, lower], axis=0)

    receive(home_pix, False)
    patches = gather_home(
        back_pix, got_pix_side, got_pix_low, got_pix_corner, got_pix_high
    )
    patches = jnp.concatenate([patches[a] for a in range(ROWS)], axis=1)
    patches = jnp.concatenate(
        [jnp.where(j_of_lane == j, patches, 0.0) for j in range(4)], axis=0
    ).astype(BF16)
    by_pixel = mm_t(place, patches).astype(BF16)
    field = mm(by_pixel, spread)
    field_ref[...] = field.reshape(VARS, 4 * ROWS, 4 * COLS).astype(BF16)

    receive(home_grad, False)
    grad_ref[...] = gather_home(
        back_grad, got_grad_side, got_grad_low, got_grad_corner, got_grad_high
    ).astype(BF16)

    sent(out_tok, True)
    sent(out_pix, True)
    sent(home_pix, False)
    sent(home_grad, False)


def per_device(lats, lons, *args):
    tokens, _, _, table, index, region = args[:6]
    cot = args[-1]
    operands = (*args[:9], args[9].T, args[10].T, cot)
    scratch = [
        pltpu.VMEM((TALL, WIDE, C), BF16),
        pltpu.VMEM((TALL, WIDE, PIX), BF16),
        pltpu.VMEM((TALL, WIDE, PIX), BF16),
        pltpu.VMEM((TALL, WIDE, C), BF16),
    ]
    for width in (PIX, C):
        scratch += [
            pltpu.VMEM((ROWS, PAD, width), BF16),
            pltpu.VMEM((HALF, 2 * PAD, width), BF16),
            pltpu.VMEM((HALF, PAD, width), BF16),
            pltpu.VMEM((HALF, 2 * PAD, width), BF16),
        ]
    scratch += [
        pltpu.VMEM((C,), F32),
        pltpu.VMEM((C,), F32),
        pltpu.VMEM((C, 3 * C), BF16),
        pltpu.VMEM((2,) + table.shape[1:], F32),
        pltpu.VMEM(index.shape, I32),
        pltpu.SMEM(region.shape, I32),
        pltpu.VMEM((C, C), BF16),
        pltpu.VMEM((C, MLP), BF16),
        pltpu.VMEM((C, MLP), BF16),
        pltpu.VMEM((16 * VARS, C), BF16),
        pltpu.VMEM(cot.shape, BF16),
        pltpu.VMEM((2, FRONT + 41 * LANES + LANES), I32),
        pltpu.VMEM((2, LANES, LANES), I32),
        pltpu.VMEM((2, HEADS, SIDE, SIDE), F32),
        pltpu.VMEM((TOKENS, MLP), F32),
        pltpu.VMEM((TOKENS, MLP), BF16),
        pltpu.VMEM((TOKENS, MLP), F32),
        pltpu.VMEM((4, HEADS, SIDE, SIDE), F32),
        pltpu.SemaphoreType.DMA((12,)),
        pltpu.SemaphoreType.DMA((16,)),
        pltpu.SemaphoreType.DMA((16,)),
    ]
    field, grad = pl.pallas_call(
        functools.partial(kernel, lats, lons),
        out_shape=(
            pltpu.VMEM(cot.shape, BF16),
            pltpu.VMEM(tokens.shape, BF16),
        ),
        in_specs=[pl.BlockSpec(memory_space=pltpu.HBM)] * 12,
        out_specs=(
            pl.BlockSpec(memory_space=pltpu.VMEM),
            pl.BlockSpec(memory_space=pltpu.VMEM),
        ),
        scratch_shapes=scratch,
        compiler_params=pltpu.CompilerParams(
            collective_id=0, has_side_effects=True, vmem_limit_bytes=40 * 1024 * 1024
        ),
    )(*(pltpu.with_memory_space_constraint(x, pltpu.HBM) for x in operands))
    return field, grad


def solution(mesh):
    return jax.shard_map(
        functools.partial(per_device, mesh.shape["lat"], mesh.shape["lon"]),
        mesh=mesh,
        in_specs=(P("lat", "lon", None),) + (P(),) * 10 + (P(None, "lat", "lon"),),
        out_specs=(P(None, "lat", "lon"), P("lat", "lon", None)),
        check_vma=False,
    )
```

```python
import functools
import math

import jax
import jax.numpy as jnp
from jax import lax
from jax.experimental import pallas as pl
from jax.experimental.pallas import tpu as pltpu
from jax.sharding import PartitionSpec as P

F32 = jnp.float32
BF16 = jnp.bfloat16
I32 = jnp.int32
MESH = pl.DeviceIdType.MESH

WLAT = 6
WLON = 12
SIDE = WLAT * WLON
ROOM = 80
HEADS = 6
DEPTH = 32
C = HEADS * DEPTH
MLP = 768
VARS = 5
ROWS = 6
COLS = 48
HALF = WLAT // 2
PAD = 16
WIDE = COLS + PAD
TALL = 2 * WLAT
SLOTS_PER_BAND = 2
BAND = SLOTS_PER_BAND * ROOM
TOKENS = 2 * BAND
LANES = 128
GROUP = 32
PIX = 4 * GROUP
EPS = 1e-05
LOG2E = math.log2(math.e)
SCALE = 1.0 / math.sqrt(DEPTH)
MASKED = -1.0e9
FRONT = LANES
GROUPS = ((0, 4), (4, 6))


def mm(a, b):
    return lax.dot_general(a, b, (((1,), (0,)), ((), ())), preferred_element_type=F32)


def mm_t(a, b):
    return lax.dot_general(a, b, (((1,), (1,)), ((), ())), preferred_element_type=F32)


def mm_tl(a, b):
    return lax.dot_general(a, b, (((0,), (0,)), ((), ())), preferred_element_type=F32)


def iota(shape, dim):
    return lax.broadcasted_iota(I32, shape, dim)


def one_hot(mask):
    return jnp.where(mask, 1.0, 0.0).astype(BF16)


def div12(t):
    return lax.shift_right_logical(t * 171, 11)


def div48(t):
    return jnp.where(t >= 144, 3, jnp.where(t >= 96, 2, jnp.where(t >= 48, 1, 0)))


def band_cells(t, upper, edge):
    slot = jnp.where(t >= ROOM, 1, 0)
    t = t - ROOM * slot
    i = div12(t)
    j = t - WLON * i
    left = (PAD - WLON // 2) + WLON * slot + j
    right = left + 2 * WLON
    if upper:
        usual = i * WIDE + left
        other = (i + HALF) * WIDE + right
        at_edge = jnp.logical_and(edge, i < HALF)
    else:
        usual = i * WIDE + right
        other = (i - HALF) * WIDE + left
        at_edge = jnp.logical_and(edge, i >= HALF)
    return jnp.where(t < SIDE, jnp.where(at_edge, other, usual), -1)


def mean_of(x):
    return jnp.sum(x, axis=-1, keepdims=True) * (1.0 / C)


def norm(x, gain):
    centered = x - mean_of(x)
    rstd = lax.rsqrt(mean_of(centered * centered) + EPS)
    xhat = centered * rstd
    return xhat, rstd, xhat * gain


def norm_back(d_out, xhat, rstd, gain):
    d_hat = d_out * gain
    return rstd * (d_hat - mean_of(d_hat) - xhat * mean_of(d_hat * xhat))


def gelu_parts(u):
    bell = jnp.exp2(u * u * (-0.5 * LOG2E))
    t = 1.0 / (1.0 + (0.3275911 * math.sqrt(0.5)) * jnp.abs(u))
    poly = t * (
        0.5 * 0.254829592
        + t
        * (
            0.5 * -0.284496736
            + t * (0.5 * 1.421413741 + t * (0.5 * -1.453152027 + t * (0.5 * 1.061405429)))
        )
    )
    tail = poly * bell
    cdf = jnp.where(u >= 0, 1.0 - tail, tail)
    return u * cdf, cdf + u * bell * (1.0 / math.sqrt(2.0 * math.pi))


def kernel(
    lats,
    lons,
    tok_hbm,
    g1_hbm,
    wqkv_hbm,
    table_hbm,
    index_hbm,
    region_hbm,
    wproj_hbm,
    g2_hbm,
    fc1_hbm,
    fc2_hbm,
    rec_hbm,
    cot_hbm,
    field_ref,
    grad_ref,
    ext_tok,
    ext_pix,
    back_pix,
    back_grad,
    got_pix_side,
    got_pix_low,
    got_pix_corner,
    got_pix_high,
    got_grad_side,
    got_grad_low,
    got_grad_corner,
    got_grad_high,
    g1_v,
    g2_v,
    wqkv,
    table,
    index,
    region,
    wproj,
    fc1,
    fc2,
    rec,
    cot,
    index_rows,
    index_square,
    bias,
    local_sem,
    send_sem,
    recv_sem,
):
    lat = lax.axis_index("lat")
    lon = lax.axis_index("lon")
    first = lat == 0
    last = lat == lats - 1
    right = lax.rem(lon + 1, lons)
    left = lax.rem(lon + lons - 1, lons)
    above = lat - 1
    below = lat + 1

    barrier = pltpu.get_barrier_semaphore()

    def greet(row, column):
        pl.semaphore_signal(barrier, inc=1, device_id=(row, column), device_id_type=MESH)

    greet(lat, left)
    greet(lat, right)

    @pl.when(jnp.logical_not(first))
    def _():
        greet(above, lon)
        greet(above, left)

    @pl.when(jnp.logical_not(last))
    def _():
        greet(below, lon)
        greet(below, right)

    def local(src, dst, number):
        copy = pltpu.make_async_copy(src, dst, local_sem.at[number])
        copy.start()
        return copy

    cot_copy = local(cot_hbm, cot, 0)
    own_copy = local(tok_hbm, ext_tok.at[HALF : HALF + ROWS, PAD:WIDE], 1)
    index_copy = local(index_hbm, index, 2)
    table_copy = local(table_hbm.at[pl.ds(lat, 2)], table, 3)
    region_copy = local(region_hbm, region, 4)
    g1_copy = local(g1_hbm, g1_v, 5)
    wqkv_copy = local(wqkv_hbm, wqkv, 6)
    wproj_copy = local(wproj_hbm, wproj, 7)
    g2_copy = local(g2_hbm, g2_v, 8)
    fc1_copy = local(fc1_hbm, fc1, 9)
    fc2_copy = local(fc2_hbm, fc2, 10)
    rec_copy = local(rec_hbm, rec, 11)

    def remote(src, dst, number, row, column):
        return pltpu.make_async_remote_copy(
            src_ref=src,
            dst_ref=dst,
            send_sem=send_sem.at[number],
            recv_sem=recv_sem.at[number],
            device_id=(row, column),
            device_id_type=MESH,
        )

    def outward(src, ext, base):
        side = remote(
            src(slice(0, ROWS), slice(COLS - PAD, COLS)),
            ext.at[HALF : HALF + ROWS, 0:PAD],
            base,
            lat,
            right,
        )
        low = remote(
            src(slice(HALF, ROWS), slice(0, 2 * PAD)),
            ext.at[0:HALF, PAD : 3 * PAD],
            base + 1,
            below,
            lon,
        )
        corner = remote(
            src(slice(HALF, ROWS), slice(COLS - PAD, COLS)),
            ext.at[0:HALF, 0:PAD],
            base + 2,
            below,
            right,
        )
        high = remote(
            src(slice(0, HALF), slice(PAD, COLS)),
            ext.at[HALF + ROWS : TALL, 2 * PAD : WIDE],
            base + 3,
            above,
            lon,
        )
        return side, low, corner, high

    def homeward(ext, side_ref, low_ref, corner_ref, high_ref, base):
        side = remote(ext.at[HALF : HALF + ROWS, 0:PAD], side_ref, base, lat, left)
        low = remote(ext.at[0:HALF, PAD : 3 * PAD], low_ref, base + 1, above, lon)
        corner = remote(ext.at[0:HALF, 0:PAD], corner_ref, base + 2, above, left)
        high = remote(
            ext.at[HALF + ROWS : TALL, 2 * PAD : WIDE], high_ref, base + 3, below, lon
        )
        return side, low, corner, high

    def send(copies, down):
        side, low, corner, high = copies
        goes, comes = (last, first) if down else (first, last)
        side.start()

        @pl.when(jnp.logical_not(goes))
        def _():
            low.start()
            corner.start()

        @pl.when(jnp.logical_not(comes))
        def _():
            high.start()

    def receive(copies, down):
        side, low, corner, high = copies
        goes, comes = (last, first) if down else (first, last)
        side.wait_recv()

        @pl.when(jnp.logical_not(comes))
        def _():
            low.wait_recv()
            corner.wait_recv()

        @pl.when(jnp.logical_not(goes))
        def _():
            high.wait_recv()

    def sent(copies, down):
        side, low, corner, high = copies
        goes, comes = (last, first) if down else (first, last)
        side.wait_send()

        @pl.when(jnp.logical_not(goes))
        def _():
            low.wait_send()
            corner.wait_send()

        @pl.when(jnp.logical_not(comes))
        def _():
            high.wait_send()

    out_tok = outward(lambda a, b: tok_hbm.at[a, b], ext_tok, 0)

    r_col = iota((4 * COLS, 1), 0)
    j_col = div48(r_col)
    spread = one_hot(iota((4 * COLS, 4 * COLS), 1) == 4 * (r_col - COLS * j_col) + j_col)
    c_row = iota((1, ROWS * PIX), 1)
    a_row = lax.shift_right_logical(c_row, 7)
    vi_row = jnp.bitwise_and(c_row, GROUP - 1)
    v_row = lax.shift_right_logical(vi_row, 2)
    pix_row = jnp.where(
        vi_row < 4 * VARS, v_row * (4 * ROWS) + 4 * a_row + jnp.bitwise_and(vi_row, 3), -1
    )
    place = one_hot(iota((4 * VARS * ROWS, ROWS * PIX), 0) == pix_row)
    j_of_lane = jnp.bitwise_and(lax.shift_right_logical(c_row, 5), 3)

    chosen = []
    chosen_t = []
    for band in range(2):
        edge = first if band == 0 else last
        cells = band_cells(iota((BAND, 1), 0), band == 0, edge)
        chosen.append(one_hot(iota((BAND, WLAT * WIDE), 1) == cells))
        cells = band_cells(iota((1, BAND), 1), band == 0, edge)
        chosen_t.append(one_hot(iota((WLAT * WIDE, BAND), 0) == cells))

    for ext in (ext_tok, ext_pix):
        ext[0:HALF, 3 * PAD : WIDE] = jnp.zeros((HALF, PAD, ext.shape[2]), BF16)
        ext[HALF + ROWS : TALL, 0 : 2 * PAD] = jnp.zeros((HALF, 2 * PAD, ext.shape[2]), BF16)

        @pl.when(first)
        def _():
            ext[0:HALF, 0 : 3 * PAD] = jnp.zeros((HALF, 3 * PAD, ext.shape[2]), BF16)

        @pl.when(last)
        def _():
            ext[HALF + ROWS : TALL, 2 * PAD : WIDE] = jnp.zeros(
                (HALF, 2 * PAD, ext.shape[2]), BF16
            )

    cot_copy.wait()
    pixels = cot[...].astype(F32).reshape(4 * VARS * ROWS, 4 * COLS).astype(BF16)
    by_column = mm_t(spread, pixels).astype(BF16)
    grouped = mm(by_column, place)
    by_token = jnp.zeros((COLS, ROWS * PIX), F32)
    for j in range(4):
        by_token = jnp.where(j_of_lane == j, grouped[j * COLS : (j + 1) * COLS], by_token)
    by_token = by_token.astype(BF16)
    for a in range(ROWS):
        ext_pix[HALF + a, PAD:WIDE, :] = by_token[:, a * PIX : (a + 1) * PIX]

    out_pix = outward(
        lambda a, b: ext_pix.at[
            slice(HALF + a.start, HALF + a.stop), slice(PAD + b.start, PAD + b.stop)
        ],
        ext_pix,
        4,
    )
    pl.semaphore_wait(barrier, 6 - 2 * jnp.where(first, 1, 0) - 2 * jnp.where(last, 1, 0))
    send(out_tok, True)
    send(out_pix, True)

    index_copy.wait()
    index_rows[...] = jnp.zeros(index_rows.shape, I32)
    index_square[...] = jnp.zeros(index_square.shape, I32)
    pairs = SIDE * SIDE
    for band in range(2):
        index_rows[band : band + 1, FRONT : FRONT + pairs] = index[pl.ds(lat + band, 1), :]
    for t in range(SIDE):
        start = FRONT + SIDE * t
        usual = index_rows[:, start : start + SIDE]
        upper = usual[0:1]
        lower = usual[1:2]
        if t < SIDE // 2:
            start = FRONT + SIDE * (t + SIDE // 2) + SIDE // 2
            upper = jnp.where(first, index_rows[0:1, start : start + SIDE], upper)
        else:
            start = FRONT + SIDE * (t - SIDE // 2) - SIDE // 2
            lower = jnp.where(last, index_rows[1:2, start : start + SIDE], lower)
        index_square[0, t : t + 1, 0:SIDE] = upper
        index_square[1, t : t + 1, 0:SIDE] = lower

    table_copy.wait()
    region_copy.wait()
    k_col = iota((SIDE, 1), 0)
    q_row = iota((1, LANES), 1)
    i_col = div12(k_col)
    i_row = div12(q_row)
    slot_count = table.shape[2]

    def table_part(band, h, c):
        stop = min(slot_count, (c + 1) * LANES)
        part = table[band, h : h + 1, c * LANES : stop]
        if stop - c * LANES < LANES:
            part = jnp.concatenate(
                [part, jnp.zeros((1, LANES - (stop - c * LANES)), F32)], axis=1
            )
        return part

    for band in range(2):
        code_col = jnp.zeros((SIDE, 1), I32)
        code_row = jnp.zeros((1, LANES), I32)
        for i in range(WLAT):
            row = WLAT * lat - HALF + WLAT * band + i
            if band == 0 and i < HALF:
                row = row + jnp.where(first, HALF, 0)
            if band == 1 and i >= HALF:
                row = row - jnp.where(last, HALF, 0)
            code = region[row]
            if band == 0 and i < HALF:
                code = code + jnp.where(first, 1000, 0)
            if band == 1 and i < HALF:
                code = code + jnp.where(last, 1000, 0)
            code_col = jnp.where(i_col == i, code, code_col)
            code_row = jnp.where(i_row == i, code, code_row)
        allowed = code_col == code_row
        square = index_square[band].T[0:SIDE]
        lane = jnp.bitwise_and(square, LANES - 1)
        chunk = lax.shift_right_logical(square, 7)
        entries = [
            [
                jnp.broadcast_to(table_part(band, h, c), (8, LANES))
                for c in range(-(-slot_count // LANES))
            ]
            for h in range(HEADS)
        ]
        for r in range(0, SIDE, 8):
            for h in range(HEADS):
                picked = jnp.zeros((8, LANES), F32)
                for c, part in enumerate(entries[h]):
                    found = jnp.take_along_axis(
                        part, lane[r : r + 8], axis=1, mode="promise_in_bounds"
                    )
                    picked = jnp.where(chunk[r : r + 8] == c, found, picked)
                bias[band, h, r : r + 8, :] = jnp.where(
                    allowed[r : r + 8], picked * LOG2E, MASKED
                )[:, 0:ROOM]
        for h in range(HEADS):
            bias[band, h, SIDE:ROOM, :] = jnp.full((ROOM - SIDE, ROOM), MASKED, F32)

    def to_windows(ext):
        width = ext.shape[2]
        return jnp.concatenate(
            [
                mm(
                    chosen[band],
                    ext[band * WLAT : (band + 1) * WLAT].reshape(WLAT * WIDE, width),
                )
                for band in range(2)
            ],
            axis=0,
        )

    def to_grid(values, ext):
        width = ext.shape[2]
        for band in range(2):
            ext[band * WLAT : (band + 1) * WLAT] = (
                mm(chosen_t[band], values[band * BAND : (band + 1) * BAND])
                .astype(BF16)
                .reshape(WLAT, WIDE, width)
            )

    g1_copy.wait()
    g2_copy.wait()
    wqkv_copy.wait()
    wproj_copy.wait()
    fc1_copy.wait()
    fc2_copy.wait()
    rec_copy.wait()
    own_copy.wait()
    gain1 = g1_v[...].reshape(1, C)
    gain2 = g2_v[...].reshape(1, C)

    c_lane = iota((PIX, 1), 0)
    vi_lane = jnp.bitwise_and(c_lane, GROUP - 1)
    source = (
        16 * lax.shift_right_logical(vi_lane, 2)
        + 4 * jnp.bitwise_and(vi_lane, 3)
        + lax.shift_right_logical(c_lane, 5)
    )
    source = jnp.where(vi_lane < 4 * VARS, source, -1)
    source = one_hot(iota((PIX, 16 * VARS), 1) == source)
    rec_wide = mm(source, rec[...]).astype(BF16)

    head_of_lane = lax.shift_right_logical(iota((1, LANES), 1), 5)
    head_masks = [jnp.where(head_of_lane == h, 1.0, 0.0).astype(BF16) for h in range(4)]

    receive(out_tok, True)
    tokens = to_windows(ext_tok)

    xhat1, rstd1, normed = norm(tokens, gain1)
    normed = normed.astype(BF16)
    wq = wqkv[:, 0:C]
    wk = wqkv[:, C : 2 * C]
    wv = wqkv[:, 2 * C : 3 * C]
    query = mm(normed, wq).astype(BF16)
    key = mm(normed, wk).astype(BF16)
    value = mm(normed, wv).astype(BF16)

    def lanes_of(x, slot, group):
        low = GROUPS[group][0] * DEPTH
        return x[slot * ROOM : (slot + 1) * ROOM, low : GROUPS[group][1] * DEPTH]

    def stack(x):
        width = x.shape[1]
        return jnp.concatenate([x * head_masks[h][:, 0:width] for h in range(width // DEPTH)])

    def by_head(x):
        heads = x.shape[0] // ROOM
        lane_head = head_of_lane[:, 0 : x.shape[1]]
        out = x[(heads - 1) * ROOM :]
        for h in range(heads - 2, -1, -1):
            out = jnp.where(lane_head == h, x[h * ROOM : (h + 1) * ROOM], out)
        return out

    def join(parts):
        return jnp.concatenate(
            [jnp.concatenate([p.astype(BF16) for p in pair], axis=1) for pair in parts], axis=0
        )

    stacks = {}
    kept = {}
    attended = []
    for slot in range(4):
        pair = []
        for group, (h0, h1) in enumerate(GROUPS):
            key_stack = stack(lanes_of(key, slot, group))
            value_stack = stack(lanes_of(value, slot, group))
            stacks[slot, group] = key_stack, value_stack
            scores = mm_t(key_stack, lanes_of(query, slot, group))
            parts = []
            for h in range(h0, h1):
                n = (h - h0) * ROOM
                s = scores[n : n + ROOM] * (SCALE * LOG2E) + bias[slot // 2, h]
                s = jnp.exp2(s - jnp.max(s, axis=0, keepdims=True))
                p = s * (1.0 / jnp.sum(s, axis=0, keepdims=True))
                kept[slot, h] = p
                parts.append(p.astype(BF16))
            weights = jnp.concatenate(parts, axis=0)
            kept[slot, group, "all"] = weights
            pair.append(mm_tl(weights, value_stack))
        attended.append(pair)
    attended = join(attended)

    resid = (tokens + mm(attended, wproj[...])).astype(BF16)
    xhat2, rstd2, normed2 = norm(resid.astype(F32), gain2)
    hidden, slope = gelu_parts(mm(normed2.astype(BF16), fc1[...]))
    hidden = hidden.astype(BF16)
    block_out = (resid.astype(F32) + mm_t(hidden, fc2[...])).astype(BF16)
    to_grid(mm_t(block_out, rec_wide).astype(BF16), back_pix)
    home_pix = homeward(
        back_pix, got_pix_side, got_pix_low, got_pix_corner, got_pix_high, 8
    )
    send(home_pix, False)

    receive(out_pix, True)
    d_block = mm(to_windows(ext_pix).astype(BF16), rec_wide).astype(BF16)
    d_hidden = mm(d_block, fc2[...]).astype(BF16).astype(F32)
    d_hidden = (d_hidden * slope).astype(BF16)
    d_normed2 = mm_t(d_hidden, fc1[...]).astype(BF16).astype(F32)
    d_resid = (
        d_block.astype(F32) + norm_back(d_normed2, xhat2, rstd2, gain2).astype(BF16).astype(F32)
    ).astype(BF16)
    d_attended = mm_t(d_resid, wproj[...]).astype(BF16)

    d_query = []
    d_key = []
    d_value = []
    for slot in range(4):
        pairs = [], [], []
        for group, (h0, h1) in enumerate(GROUPS):
            key_stack, value_stack = stacks[slot, group]
            d_out = lanes_of(d_attended, slot, group)
            d_weights = mm_t(value_stack, d_out)
            parts = []
            for h in range(h0, h1):
                n = (h - h0) * ROOM
                p = kept[slot, h]
                pd = p * d_weights[n : n + ROOM]
                d = (pd - p * jnp.sum(pd, axis=0, keepdims=True)) * SCALE
                parts.append(d.astype(BF16))
            d_scores = jnp.concatenate(parts, axis=0)
            pairs[0].append(mm_tl(d_scores, key_stack))
            pairs[1].append(by_head(mm(d_scores, lanes_of(query, slot, group))))
            pairs[2].append(by_head(mm(kept[slot, group, "all"], d_out)))
        d_query.append(pairs[0])
        d_key.append(pairs[1])
        d_value.append(pairs[2])
    d_query, d_key, d_value = join(d_query), join(d_key), join(d_value)

    d_normed = mm_t(d_query, wq) + mm_t(d_key, wk) + mm_t(d_value, wv)
    d_normed = d_normed.astype(BF16).astype(F32)
    through = norm_back(d_normed, xhat1, rstd1, gain1).astype(BF16).astype(F32)
    to_grid((d_resid.astype(F32) + through).astype(BF16), back_grad)
    home_grad = homeward(
        back_grad, got_grad_side, got_grad_low, got_grad_corner, got_grad_high, 12
    )
    send(home_grad, False)

    def gather_home(ext, side, low, corner, high):
        width = ext.shape[2]
        own = ext[HALF : HALF + ROWS, PAD:WIDE, :].astype(F32)
        from_side = side[...].astype(F32)
        from_low = jnp.where(last, 0.0, low[...].astype(F32))
        from_corner = jnp.where(last, 0.0, corner[...].astype(F32))
        from_high = jnp.where(first, 0.0, high[...].astype(F32))
        upper = jnp.concatenate(
            [
                own[0:HALF, 0:PAD],
                own[0:HALF, PAD : 2 * PAD] + from_high[:, 0:PAD],
                own[0:HALF, 2 * PAD :] + from_high[:, PAD:] + from_side[0:HALF],
            ],
            axis=1,
        )
        lower = jnp.concatenate(
            [
                own[HALF:, 0 : 2 * PAD] + from_low,
                own[HALF:, 2 * PAD :] + from_corner + from_side[HALF:],
            ],
            axis=1,
        )
        return jnp.concatenate([upper, lower], axis=0)

    receive(home_pix, False)
    patches = gather_home(
        back_pix, got_pix_side, got_pix_low, got_pix_corner, got_pix_high
    )
    patches = jnp.concatenate([patches[a] for a in range(ROWS)], axis=1)
    patches = jnp.concatenate(
        [jnp.where(j_of_lane == j, patches, 0.0) for j in range(4)], axis=0
    ).astype(BF16)
    by_pixel = mm_t(place, patches).astype(BF16)
    field = mm(by_pixel, spread)
    field_ref[...] = field.reshape(VARS, 4 * ROWS, 4 * COLS).astype(BF16)

    receive(home_grad, False)
    grad_ref[...] = gather_home(
        back_grad, got_grad_side, got_grad_low, got_grad_corner, got_grad_high
    ).astype(BF16)

    sent(out_tok, True)
    sent(out_pix, True)
    sent(home_pix, False)
    sent(home_grad, False)


def put_kernel(a_ref, b_ref, a_out, b_out, sem):
    copies = [
        pltpu.make_async_copy(a_ref, a_out, sem.at[0]),
        pltpu.make_async_copy(b_ref, b_out, sem.at[1]),
    ]
    for copy in copies:
        copy.start()
    for copy in copies:
        copy.wait()


def put(a, b):
    return pl.pallas_call(
        put_kernel,
        out_shape=(pltpu.HBM(a.shape, a.dtype), pltpu.HBM(b.shape, b.dtype)),
        in_specs=[pl.BlockSpec(memory_space=pltpu.VMEM)] * 2,
        out_specs=(pl.BlockSpec(memory_space=pl.ANY), pl.BlockSpec(memory_space=pl.ANY)),
        scratch_shapes=[pltpu.SemaphoreType.DMA((2,))],
    )(pltpu.with_memory_space_constraint(a, pltpu.VMEM), pltpu.with_memory_space_constraint(b, pltpu.VMEM))


def per_device(lats, lons, *args):
    tokens, _, _, table, index, region = args[:6]
    cot = args[-1]
    operands = (*args[:9], args[9].T, args[10].T, cot)
    scratch = [
        pltpu.VMEM((TALL, WIDE, C), BF16),
        pltpu.VMEM((TALL, WIDE, PIX), BF16),
        pltpu.VMEM((TALL, WIDE, PIX), BF16),
        pltpu.VMEM((TALL, WIDE, C), BF16),
    ]
    for width in (PIX, C):
        scratch += [
            pltpu.VMEM((ROWS, PAD, width), BF16),
            pltpu.VMEM((HALF, 2 * PAD, width), BF16),
            pltpu.VMEM((HALF, PAD, width), BF16),
            pltpu.VMEM((HALF, 2 * PAD, width), BF16),
        ]
    scratch += [
        pltpu.VMEM((C,), F32),
        pltpu.VMEM((C,), F32),
        pltpu.VMEM((C, 3 * C), BF16),
        pltpu.VMEM((2,) + table.shape[1:], F32),
        pltpu.VMEM(index.shape, I32),
        pltpu.SMEM(region.shape, I32),
        pltpu.VMEM((C, C), BF16),
        pltpu.VMEM((C, MLP), BF16),
        pltpu.VMEM((C, MLP), BF16),
        pltpu.VMEM((16 * VARS, C), BF16),
        pltpu.VMEM(cot.shape, BF16),
        pltpu.VMEM((2, FRONT + 41 * LANES + LANES), I32),
        pltpu.VMEM((2, LANES, LANES), I32),
        pltpu.VMEM((2, HEADS, ROOM, ROOM), F32),
        pltpu.SemaphoreType.DMA((12,)),
        pltpu.SemaphoreType.DMA((16,)),
        pltpu.SemaphoreType.DMA((16,)),
    ]
    field, grad = pl.pallas_call(
        functools.partial(kernel, lats, lons),
        out_shape=(
            pltpu.VMEM(cot.shape, BF16),
            pltpu.VMEM(tokens.shape, BF16),
        ),
        in_specs=[pl.BlockSpec(memory_space=pltpu.HBM)] * 12,
        out_specs=(
            pl.BlockSpec(memory_space=pltpu.VMEM),
            pl.BlockSpec(memory_space=pltpu.VMEM),
        ),
        scratch_shapes=scratch,
        compiler_params=pltpu.CompilerParams(
            collective_id=0, has_side_effects=True, vmem_limit_bytes=40 * 1024 * 1024
        ),
    )(*(pltpu.with_memory_space_constraint(x, pltpu.HBM) for x in operands))
    return put(field, grad)


def solution(mesh):
    return jax.shard_map(
        functools.partial(per_device, mesh.shape["lat"], mesh.shape["lon"]),
        mesh=mesh,
        in_specs=(P("lat", "lon", None),) + (P(),) * 10 + (P(None, "lat", "lon"),),
        out_specs=(P(None, "lat", "lon"), P("lat", "lon", None)),
        check_vma=False,
    )
```

```python
import functools
import math

import jax
import jax.numpy as jnp
from jax import lax
from jax.experimental import pallas as pl
from jax.experimental.pallas import tpu as pltpu
from jax.sharding import PartitionSpec as P

F32 = jnp.float32
BF16 = jnp.bfloat16
I32 = jnp.int32
MESH = pl.DeviceIdType.MESH

WLAT = 6
WLON = 12
SIDE = WLAT * WLON
ROOM = 80
HEADS = 6
DEPTH = 32
C = HEADS * DEPTH
MLP = 768
VARS = 5
ROWS = 6
COLS = 48
HALF = WLAT // 2
PAD = 16
WIDE = COLS + PAD
TALL = 2 * WLAT
SLOTS_PER_BAND = 2
BAND = SLOTS_PER_BAND * ROOM
TOKENS = 2 * BAND
LANES = 128
GROUP = 32
PIX = 4 * GROUP
EPS = 1e-05
LOG2E = math.log2(math.e)
SCALE = 1.0 / math.sqrt(DEPTH)
MASKED = -1.0e9
FRONT = LANES
GROUPS = ((0, 4), (4, 6))


def mm(a, b):
    return lax.dot_general(a, b, (((1,), (0,)), ((), ())), preferred_element_type=F32)


def mm_t(a, b):
    return lax.dot_general(a, b, (((1,), (1,)), ((), ())), preferred_element_type=F32)


def mm_tl(a, b):
    return lax.dot_general(a, b, (((0,), (0,)), ((), ())), preferred_element_type=F32)


def iota(shape, dim):
    return lax.broadcasted_iota(I32, shape, dim)


def one_hot(mask):
    return jnp.where(mask, 1.0, 0.0).astype(BF16)


def div12(t):
    return lax.shift_right_logical(t * 171, 11)


def div48(t):
    return jnp.where(t >= 144, 3, jnp.where(t >= 96, 2, jnp.where(t >= 48, 1, 0)))


def band_cells(t, upper, edge):
    slot = jnp.where(t >= ROOM, 1, 0)
    t = t - ROOM * slot
    i = div12(t)
    j = t - WLON * i
    left = (PAD - WLON // 2) + WLON * slot + j
    right = left + 2 * WLON
    if upper:
        usual = i * WIDE + left
        other = (i + HALF) * WIDE + right
        at_edge = jnp.logical_and(edge, i < HALF)
    else:
        usual = i * WIDE + right
        other = (i - HALF) * WIDE + left
        at_edge = jnp.logical_and(edge, i >= HALF)
    return jnp.where(t < SIDE, jnp.where(at_edge, other, usual), -1)


def mean_of(x):
    return jnp.sum(x, axis=-1, keepdims=True) * (1.0 / C)


def norm(x, gain):
    centered = x - mean_of(x)
    rstd = lax.rsqrt(mean_of(centered * centered) + EPS)
    xhat = centered * rstd
    return xhat, rstd, xhat * gain


def norm_back(d_out, xhat, rstd, gain):
    d_hat = d_out * gain
    return rstd * (d_hat - mean_of(d_hat) - xhat * mean_of(d_hat * xhat))


def gelu_parts(u):
    bell = jnp.exp2(u * u * (-0.5 * LOG2E))
    t = 1.0 / (1.0 + (0.3275911 * math.sqrt(0.5)) * jnp.abs(u))
    poly = t * (
        0.5 * 0.254829592
        + t
        * (
            0.5 * -0.284496736
            + t * (0.5 * 1.421413741 + t * (0.5 * -1.453152027 + t * (0.5 * 1.061405429)))
        )
    )
    tail = poly * bell
    cdf = jnp.where(u >= 0, 1.0 - tail, tail)
    return u * cdf, cdf + u * bell * (1.0 / math.sqrt(2.0 * math.pi))


def kernel(
    lats,
    lons,
    tok_hbm,
    g1_hbm,
    wqkv_hbm,
    table_hbm,
    index_hbm,
    region_hbm,
    wproj_hbm,
    g2_hbm,
    fc1_hbm,
    fc2_hbm,
    rec_hbm,
    cot_hbm,
    field_ref,
    grad_ref,
    ext_tok,
    ext_pix,
    back_pix,
    back_grad,
    got_pix_side,
    got_pix_low,
    got_pix_corner,
    got_pix_high,
    got_grad_side,
    got_grad_low,
    got_grad_corner,
    got_grad_high,
    g1_v,
    g2_v,
    wqkv,
    table,
    index,
    region,
    wproj,
    fc1,
    fc2,
    rec,
    cot,
    index_rows,
    index_square,
    bias,
    local_sem,
    send_sem,
    recv_sem,
):
    lat = lax.axis_index("lat")
    lon = lax.axis_index("lon")
    first = lat == 0
    last = lat == lats - 1
    right = lax.rem(lon + 1, lons)
    left = lax.rem(lon + lons - 1, lons)
    above = lat - 1
    below = lat + 1

    barrier = pltpu.get_barrier_semaphore()

    def greet(row, column):
        pl.semaphore_signal(barrier, inc=1, device_id=(row, column), device_id_type=MESH)

    greet(lat, left)
    greet(lat, right)

    @pl.when(jnp.logical_not(first))
    def _():
        greet(above, lon)
        greet(above, left)

    @pl.when(jnp.logical_not(last))
    def _():
        greet(below, lon)
        greet(below, right)

    def local(src, dst, number):
        copy = pltpu.make_async_copy(src, dst, local_sem.at[number])
        copy.start()
        return copy

    own_copy = local(tok_hbm, ext_tok.at[HALF : HALF + ROWS, PAD:WIDE], 1)
    cot_copy = local(cot_hbm, cot, 0)
    index_copy = local(index_hbm, index, 2)
    table_copy = local(table_hbm.at[pl.ds(lat, 2)], table, 3)
    region_copy = local(region_hbm, region, 4)
    g1_copy = local(g1_hbm, g1_v, 5)
    wqkv_copy = local(wqkv_hbm, wqkv, 6)
    wproj_copy = local(wproj_hbm, wproj, 7)
    g2_copy = local(g2_hbm, g2_v, 8)
    fc1_copy = local(fc1_hbm, fc1, 9)
    fc2_copy = local(fc2_hbm, fc2, 10)
    rec_copy = local(rec_hbm, rec, 11)

    def remote(src, dst, number, row, column):
        return pltpu.make_async_remote_copy(
            src_ref=src,
            dst_ref=dst,
            send_sem=send_sem.at[number],
            recv_sem=recv_sem.at[number],
            device_id=(row, column),
            device_id_type=MESH,
        )

    def outward(src, ext, base):
        side = remote(
            src(slice(0, ROWS), slice(COLS - PAD, COLS)),
            ext.at[HALF : HALF + ROWS, 0:PAD],
            base,
            lat,
            right,
        )
        low = remote(
            src(slice(HALF, ROWS), slice(0, 2 * PAD)),
            ext.at[0:HALF, PAD : 3 * PAD],
            base + 1,
            below,
            lon,
        )
        corner = remote(
            src(slice(HALF, ROWS), slice(COLS - PAD, COLS)),
            ext.at[0:HALF, 0:PAD],
            base + 2,
            below,
            right,
        )
        high = remote(
            src(slice(0, HALF), slice(PAD, COLS)),
            ext.at[HALF + ROWS : TALL, 2 * PAD : WIDE],
            base + 3,
            above,
            lon,
        )
        return side, low, corner, high

    def homeward(ext, side_ref, low_ref, corner_ref, high_ref, base):
        side = remote(ext.at[HALF : HALF + ROWS, 0:PAD], side_ref, base, lat, left)
        low = remote(ext.at[0:HALF, PAD : 3 * PAD], low_ref, base + 1, above, lon)
        corner = remote(ext.at[0:HALF, 0:PAD], corner_ref, base + 2, above, left)
        high = remote(
            ext.at[HALF + ROWS : TALL, 2 * PAD : WIDE], high_ref, base + 3, below, lon
        )
        return side, low, corner, high

    def send(copies, down):
        side, low, corner, high = copies
        goes, comes = (last, first) if down else (first, last)

        @pl.when(jnp.logical_not(goes))
        def _():
            corner.start()
            low.start()

        side.start()

        @pl.when(jnp.logical_not(comes))
        def _():
            high.start()

    def receive(copies, down):
        side, low, corner, high = copies
        goes, comes = (last, first) if down else (first, last)
        side.wait_recv()

        @pl.when(jnp.logical_not(comes))
        def _():
            low.wait_recv()
            corner.wait_recv()

        @pl.when(jnp.logical_not(goes))
        def _():
            high.wait_recv()

    def sent(copies, down):
        side, low, corner, high = copies
        goes, comes = (last, first) if down else (first, last)
        side.wait_send()

        @pl.when(jnp.logical_not(goes))
        def _():
            low.wait_send()
            corner.wait_send()

        @pl.when(jnp.logical_not(comes))
        def _():
            high.wait_send()

    def own_part(ext):
        return lambda a, b: ext.at[
            slice(HALF + a.start, HALF + a.stop), slice(PAD + b.start, PAD + b.stop)
        ]

    out_tok = outward(own_part(ext_tok), ext_tok, 0)

    r_col = iota((4 * COLS, 1), 0)
    j_col = div48(r_col)
    spread = one_hot(iota((4 * COLS, 4 * COLS), 1) == 4 * (r_col - COLS * j_col) + j_col)
    c_row = iota((1, ROWS * PIX), 1)
    a_row = lax.shift_right_logical(c_row, 7)
    vi_row = jnp.bitwise_and(c_row, GROUP - 1)
    v_row = lax.shift_right_logical(vi_row, 2)
    pix_row = jnp.where(
        vi_row < 4 * VARS, v_row * (4 * ROWS) + 4 * a_row + jnp.bitwise_and(vi_row, 3), -1
    )
    place = one_hot(iota((4 * VARS * ROWS, ROWS * PIX), 0) == pix_row)
    j_of_lane = jnp.bitwise_and(lax.shift_right_logical(c_row, 5), 3)

    chosen = []
    chosen_t = []
    for band in range(2):
        edge = first if band == 0 else last
        cells = band_cells(iota((BAND, 1), 0), band == 0, edge)
        chosen.append(one_hot(iota((BAND, WLAT * WIDE), 1) == cells))
        cells = band_cells(iota((1, BAND), 1), band == 0, edge)
        chosen_t.append(one_hot(iota((WLAT * WIDE, BAND), 0) == cells))

    for ext in (ext_tok, ext_pix):
        ext[0:HALF, 3 * PAD : WIDE] = jnp.zeros((HALF, PAD, ext.shape[2]), BF16)
        ext[HALF + ROWS : TALL, 0 : 2 * PAD] = jnp.zeros((HALF, 2 * PAD, ext.shape[2]), BF16)

        @pl.when(first)
        def _():
            ext[0:HALF, 0 : 3 * PAD] = jnp.zeros((HALF, 3 * PAD, ext.shape[2]), BF16)

        @pl.when(last)
        def _():
            ext[HALF + ROWS : TALL, 2 * PAD : WIDE] = jnp.zeros(
                (HALF, 2 * PAD, ext.shape[2]), BF16
            )

    cot_copy.wait()
    pixels = cot[...].astype(F32).reshape(4 * VARS * ROWS, 4 * COLS).astype(BF16)
    by_column = mm_t(spread, pixels).astype(BF16)
    grouped = mm(by_column, place)
    by_token = jnp.zeros((COLS, ROWS * PIX), F32)
    for j in range(4):
        by_token = jnp.where(j_of_lane == j, grouped[j * COLS : (j + 1) * COLS], by_token)
    by_token = by_token.astype(BF16)
    for a in range(ROWS):
        ext_pix[HALF + a, PAD:WIDE, :] = by_token[:, a * PIX : (a + 1) * PIX]

    out_pix = outward(own_part(ext_pix), ext_pix, 4)
    own_copy.wait()
    pl.semaphore_wait(barrier, 6 - 2 * jnp.where(first, 1, 0) - 2 * jnp.where(last, 1, 0))
    send(out_tok, True)
    send(out_pix, True)

    index_copy.wait()
    index_rows[...] = jnp.zeros(index_rows.shape, I32)
    index_square[...] = jnp.zeros(index_square.shape, I32)
    pairs = SIDE * SIDE
    for band in range(2):
        index_rows[band : band + 1, FRONT : FRONT + pairs] = index[pl.ds(lat + band, 1), :]
    for t in range(SIDE):
        start = FRONT + SIDE * t
        usual = index_rows[:, start : start + SIDE]
        upper = usual[0:1]
        lower = usual[1:2]
        if t < SIDE // 2:
            start = FRONT + SIDE * (t + SIDE // 2) + SIDE // 2
            upper = jnp.where(first, index_rows[0:1, start : start + SIDE], upper)
        else:
            start = FRONT + SIDE * (t - SIDE // 2) - SIDE // 2
            lower = jnp.where(last, index_rows[1:2, start : start + SIDE], lower)
        index_square[0, t : t + 1, 0:SIDE] = upper
        index_square[1, t : t + 1, 0:SIDE] = lower

    table_copy.wait()
    region_copy.wait()
    k_col = iota((SIDE, 1), 0)
    q_row = iota((1, LANES), 1)
    i_col = div12(k_col)
    i_row = div12(q_row)
    slot_count = table.shape[2]

    def table_part(band, h, c):
        stop = min(slot_count, (c + 1) * LANES)
        part = table[band, h : h + 1, c * LANES : stop]
        if stop - c * LANES < LANES:
            part = jnp.concatenate(
                [part, jnp.zeros((1, LANES - (stop - c * LANES)), F32)], axis=1
            )
        return part

    for band in range(2):
        code_col = jnp.zeros((SIDE, 1), I32)
        code_row = jnp.zeros((1, LANES), I32)
        for i in range(WLAT):
            row = WLAT * lat - HALF + WLAT * band + i
            if band == 0 and i < HALF:
                row = row + jnp.where(first, HALF, 0)
            if band == 1 and i >= HALF:
                row = row - jnp.where(last, HALF, 0)
            code = region[row]
            if band == 0 and i < HALF:
                code = code + jnp.where(first, 1000, 0)
            if band == 1 and i < HALF:
                code = code + jnp.where(last, 1000, 0)
            code_col = jnp.where(i_col == i, code, code_col)
            code_row = jnp.where(i_row == i, code, code_row)
        allowed = code_col == code_row
        square = index_square[band].T[0:SIDE]
        lane = jnp.bitwise_and(square, LANES - 1)
        chunk = lax.shift_right_logical(square, 7)
        entries = [
            [
                jnp.broadcast_to(table_part(band, h, c), (8, LANES))
                for c in range(-(-slot_count // LANES))
            ]
            for h in range(HEADS)
        ]
        for r in range(0, SIDE, 8):
            for h in range(HEADS):
                picked = jnp.zeros((8, LANES), F32)
                for c, part in enumerate(entries[h]):
                    found = jnp.take_along_axis(
                        part, lane[r : r + 8], axis=1, mode="promise_in_bounds"
                    )
                    picked = jnp.where(chunk[r : r + 8] == c, found, picked)
                bias[band, h, r : r + 8, :] = jnp.where(
                    allowed[r : r + 8], picked * LOG2E, MASKED
                )[:, 0:ROOM]
        for h in range(HEADS):
            bias[band, h, SIDE:ROOM, :] = jnp.full((ROOM - SIDE, ROOM), MASKED, F32)

    def to_windows(ext):
        width = ext.shape[2]
        return jnp.concatenate(
            [
                mm(
                    chosen[band],
                    ext[band * WLAT : (band + 1) * WLAT].reshape(WLAT * WIDE, width),
                )
                for band in range(2)
            ],
            axis=0,
        )

    def to_grid(values, ext):
        width = ext.shape[2]
        for band in range(2):
            ext[band * WLAT : (band + 1) * WLAT] = (
                mm(chosen_t[band], values[band * BAND : (band + 1) * BAND])
                .astype(BF16)
                .reshape(WLAT, WIDE, width)
            )

    g1_copy.wait()
    g2_copy.wait()
    wqkv_copy.wait()
    wproj_copy.wait()
    fc1_copy.wait()
    fc2_copy.wait()
    rec_copy.wait()
    gain1 = g1_v[...].reshape(1, C)
    gain2 = g2_v[...].reshape(1, C)

    c_lane = iota((PIX, 1), 0)
    vi_lane = jnp.bitwise_and(c_lane, GROUP - 1)
    source = (
        16 * lax.shift_right_logical(vi_lane, 2)
        + 4 * jnp.bitwise_and(vi_lane, 3)
        + lax.shift_right_logical(c_lane, 5)
    )
    source = jnp.where(vi_lane < 4 * VARS, source, -1)
    source = one_hot(iota((PIX, 16 * VARS), 1) == source)
    rec_wide = mm(source, rec[...]).astype(BF16)

    head_of_lane = lax.shift_right_logical(iota((1, LANES), 1), 5)
    head_masks = [jnp.where(head_of_lane == h, 1.0, 0.0).astype(BF16) for h in range(4)]

    receive(out_tok, True)
    tokens = to_windows(ext_tok)

    xhat1, rstd1, normed = norm(tokens, gain1)
    normed = normed.astype(BF16)
    wq = wqkv[:, 0:C]
    wk = wqkv[:, C : 2 * C]
    wv = wqkv[:, 2 * C : 3 * C]
    query = mm(normed, wq).astype(BF16)
    key = mm(normed, wk).astype(BF16)
    value = mm(normed, wv).astype(BF16)

    def lanes_of(x, slot, group):
        low = GROUPS[group][0] * DEPTH
        return x[slot * ROOM : (slot + 1) * ROOM, low : GROUPS[group][1] * DEPTH]

    def stack(x):
        width = x.shape[1]
        return jnp.concatenate([x * head_masks[h][:, 0:width] for h in range(width // DEPTH)])

    def by_head(x):
        heads = x.shape[0] // ROOM
        lane_head = head_of_lane[:, 0 : x.shape[1]]
        out = x[(heads - 1) * ROOM :]
        for h in range(heads - 2, -1, -1):
            out = jnp.where(lane_head == h, x[h * ROOM : (h + 1) * ROOM], out)
        return out

    def join(parts):
        return jnp.concatenate(
            [jnp.concatenate([p.astype(BF16) for p in pair], axis=1) for pair in parts], axis=0
        )

    units = [(slot, group) for slot in range(4) for group in range(len(GROUPS))]
    key_stacks = {u: stack(lanes_of(key, *u)) for u in units}
    scores = {u: mm_t(key_stacks[u], lanes_of(query, *u)) for u in units}
    value_stacks = {u: stack(lanes_of(value, *u)) for u in units}
    kept = {}
    weights = {}
    for slot, group in units:
        parts = []
        for n, h in enumerate(range(*GROUPS[group])):
            s = scores[slot, group][n * ROOM : (n + 1) * ROOM]
            s = s * (SCALE * LOG2E) + bias[slot // 2, h]
            s = jnp.exp2(s - jnp.max(s, axis=0, keepdims=True))
            p = s * (1.0 / jnp.sum(s, axis=0, keepdims=True))
            kept[slot, h] = p
            parts.append(p.astype(BF16))
        weights[slot, group] = jnp.concatenate(parts, axis=0)
    attended = {u: mm_tl(weights[u], value_stacks[u]) for u in units}
    attended = [[attended[slot, 0], attended[slot, 1]] for slot in range(4)]
    attended = join(attended)

    resid = (tokens + mm(attended, wproj[...])).astype(BF16)
    xhat2, rstd2, normed2 = norm(resid.astype(F32), gain2)
    hidden, slope = gelu_parts(mm(normed2.astype(BF16), fc1[...]))
    hidden = hidden.astype(BF16)
    block_out = (resid.astype(F32) + mm_t(hidden, fc2[...])).astype(BF16)
    to_grid(mm_t(block_out, rec_wide).astype(BF16), back_pix)
    home_pix = homeward(
        back_pix, got_pix_side, got_pix_low, got_pix_corner, got_pix_high, 8
    )
    send(home_pix, False)

    receive(out_pix, True)
    d_block = mm(to_windows(ext_pix).astype(BF16), rec_wide).astype(BF16)
    d_hidden = mm(d_block, fc2[...]).astype(BF16).astype(F32)
    d_hidden = (d_hidden * slope).astype(BF16)
    d_normed2 = mm_t(d_hidden, fc1[...]).astype(BF16).astype(F32)
    d_resid = (
        d_block.astype(F32) + norm_back(d_normed2, xhat2, rstd2, gain2).astype(BF16).astype(F32)
    ).astype(BF16)
    d_attended = mm_t(d_resid, wproj[...]).astype(BF16)

    d_outs = {u: lanes_of(d_attended, *u) for u in units}
    d_weights = {u: mm_t(value_stacks[u], d_outs[u]) for u in units}
    d_value = {u: by_head(mm(weights[u], d_outs[u])) for u in units}
    d_scores = {}
    for slot, group in units:
        parts = []
        for n, h in enumerate(range(*GROUPS[group])):
            p = kept[slot, h]
            pd = p * d_weights[slot, group][n * ROOM : (n + 1) * ROOM]
            d = (pd - p * jnp.sum(pd, axis=0, keepdims=True)) * SCALE
            parts.append(d.astype(BF16))
        d_scores[slot, group] = jnp.concatenate(parts, axis=0)
    d_query = {u: mm_tl(d_scores[u], key_stacks[u]) for u in units}
    d_key = {u: by_head(mm(d_scores[u], lanes_of(query, *u))) for u in units}
    d_query, d_key, d_value = (
        [[d[slot, 0], d[slot, 1]] for slot in range(4)] for d in (d_query, d_key, d_value)
    )
    d_query, d_key, d_value = join(d_query), join(d_key), join(d_value)

    d_normed = mm_t(d_query, wq) + mm_t(d_key, wk) + mm_t(d_value, wv)
    d_normed = d_normed.astype(BF16).astype(F32)
    through = norm_back(d_normed, xhat1, rstd1, gain1).astype(BF16).astype(F32)
    to_grid((d_resid.astype(F32) + through).astype(BF16), back_grad)
    home_grad = homeward(
        back_grad, got_grad_side, got_grad_low, got_grad_corner, got_grad_high, 12
    )
    send(home_grad, False)

    def gather_home(ext, side, low, corner, high):
        width = ext.shape[2]
        own = ext[HALF : HALF + ROWS, PAD:WIDE, :].astype(F32)
        from_side = side[...].astype(F32)
        from_low = jnp.where(last, 0.0, low[...].astype(F32))
        from_corner = jnp.where(last, 0.0, corner[...].astype(F32))
        from_high = jnp.where(first, 0.0, high[...].astype(F32))
        upper = jnp.concatenate(
            [
                own[0:HALF, 0:PAD],
                own[0:HALF, PAD : 2 * PAD] + from_high[:, 0:PAD],
                own[0:HALF, 2 * PAD :] + from_high[:, PAD:] + from_side[0:HALF],
            ],
            axis=1,
        )
        lower = jnp.concatenate(
            [
                own[HALF:, 0 : 2 * PAD] + from_low,
                own[HALF:, 2 * PAD :] + from_corner + from_side[HALF:],
            ],
            axis=1,
        )
        return jnp.concatenate([upper, lower], axis=0)

    receive(home_pix, False)
    patches = gather_home(
        back_pix, got_pix_side, got_pix_low, got_pix_corner, got_pix_high
    )
    patches = jnp.concatenate([patches[a] for a in range(ROWS)], axis=1)
    patches = jnp.concatenate(
        [jnp.where(j_of_lane == j, patches, 0.0) for j in range(4)], axis=0
    ).astype(BF16)
    by_pixel = mm_t(place, patches).astype(BF16)
    field = mm(by_pixel, spread)
    field_ref[...] = field.reshape(VARS, 4 * ROWS, 4 * COLS).astype(BF16)

    receive(home_grad, False)
    grad_ref[...] = gather_home(
        back_grad, got_grad_side, got_grad_low, got_grad_corner, got_grad_high
    ).astype(BF16)

    sent(out_tok, True)
    sent(out_pix, True)
    sent(home_pix, False)
    sent(home_grad, False)


def put_kernel(a_ref, b_ref, a_out, b_out, sem):
    copies = [
        pltpu.make_async_copy(a_ref, a_out, sem.at[0]),
        pltpu.make_async_copy(b_ref, b_out, sem.at[1]),
    ]
    for copy in copies:
        copy.start()
    for copy in copies:
        copy.wait()


def put(a, b):
    return pl.pallas_call(
        put_kernel,
        out_shape=(pltpu.HBM(a.shape, a.dtype), pltpu.HBM(b.shape, b.dtype)),
        in_specs=[pl.BlockSpec(memory_space=pltpu.VMEM)] * 2,
        out_specs=(pl.BlockSpec(memory_space=pl.ANY), pl.BlockSpec(memory_space=pl.ANY)),
        scratch_shapes=[pltpu.SemaphoreType.DMA((2,))],
    )(pltpu.with_memory_space_constraint(a, pltpu.VMEM), pltpu.with_memory_space_constraint(b, pltpu.VMEM))


def per_device(lats, lons, *args):
    tokens, _, _, table, index, region = args[:6]
    cot = args[-1]
    operands = (*args[:9], args[9].T, args[10].T, cot)
    scratch = [
        pltpu.VMEM((TALL, WIDE, C), BF16),
        pltpu.VMEM((TALL, WIDE, PIX), BF16),
        pltpu.VMEM((TALL, WIDE, PIX), BF16),
        pltpu.VMEM((TALL, WIDE, C), BF16),
    ]
    for width in (PIX, C):
        scratch += [
            pltpu.VMEM((ROWS, PAD, width), BF16),
            pltpu.VMEM((HALF, 2 * PAD, width), BF16),
            pltpu.VMEM((HALF, PAD, width), BF16),
            pltpu.VMEM((HALF, 2 * PAD, width), BF16),
        ]
    scratch += [
        pltpu.VMEM((C,), F32),
        pltpu.VMEM((C,), F32),
        pltpu.VMEM((C, 3 * C), BF16),
        pltpu.VMEM((2,) + table.shape[1:], F32),
        pltpu.VMEM(index.shape, I32),
        pltpu.SMEM(region.shape, I32),
        pltpu.VMEM((C, C), BF16),
        pltpu.VMEM((C, MLP), BF16),
        pltpu.VMEM((C, MLP), BF16),
        pltpu.VMEM((16 * VARS, C), BF16),
        pltpu.VMEM(cot.shape, BF16),
        pltpu.VMEM((2, FRONT + 41 * LANES + LANES), I32),
        pltpu.VMEM((2, LANES, LANES), I32),
        pltpu.VMEM((2, HEADS, ROOM, ROOM), F32),
        pltpu.SemaphoreType.DMA((12,)),
        pltpu.SemaphoreType.DMA((16,)),
        pltpu.SemaphoreType.DMA((16,)),
    ]
    field, grad = pl.pallas_call(
        functools.partial(kernel, lats, lons),
        out_shape=(
            pltpu.VMEM(cot.shape, BF16),
            pltpu.VMEM(tokens.shape, BF16),
        ),
        in_specs=[pl.BlockSpec(memory_space=pltpu.HBM)] * 12,
        out_specs=(
            pl.BlockSpec(memory_space=pltpu.VMEM),
            pl.BlockSpec(memory_space=pltpu.VMEM),
        ),
        scratch_shapes=scratch,
        compiler_params=pltpu.CompilerParams(
            collective_id=0, has_side_effects=True, vmem_limit_bytes=40 * 1024 * 1024
        ),
    )(*(pltpu.with_memory_space_constraint(x, pltpu.HBM) for x in operands))
    return put(field, grad)


def solution(mesh):
    return jax.shard_map(
        functools.partial(per_device, mesh.shape["lat"], mesh.shape["lon"]),
        mesh=mesh,
        in_specs=(P("lat", "lon", None),) + (P(),) * 10 + (P(None, "lat", "lon"),),
        out_specs=(P(None, "lat", "lon"), P("lat", "lon", None)),
        check_vma=False,
    )
```

```python
import functools
import math

import jax
import jax.numpy as jnp
from jax import lax
from jax.experimental import pallas as pl
from jax.experimental.pallas import tpu as pltpu
from jax.sharding import PartitionSpec as P

F32 = jnp.float32
BF16 = jnp.bfloat16
I32 = jnp.int32
MESH = pl.DeviceIdType.MESH

WLAT = 6
WLON = 12
SIDE = WLAT * WLON
ROOM = 80
HEADS = 6
DEPTH = 32
C = HEADS * DEPTH
MLP = 768
VARS = 5
ROWS = 6
COLS = 48
HALF = WLAT // 2
PAD = 16
WIDE = COLS + PAD
TALL = 2 * WLAT
SLOTS_PER_BAND = 2
BAND = SLOTS_PER_BAND * ROOM
TOKENS = 2 * BAND
LANES = 128
GROUP = 32
PIX = 4 * GROUP
EPS = 1e-05
LOG2E = math.log2(math.e)
SCALE = 1.0 / math.sqrt(DEPTH)
MASKED = -1.0e9
FRONT = LANES
GROUPS = ((0, 4), (4, 6))


def mm(a, b):
    return lax.dot_general(a, b, (((1,), (0,)), ((), ())), preferred_element_type=F32)


def mm_t(a, b):
    return lax.dot_general(a, b, (((1,), (1,)), ((), ())), preferred_element_type=F32)


def mm_tl(a, b):
    return lax.dot_general(a, b, (((0,), (0,)), ((), ())), preferred_element_type=F32)


def iota(shape, dim):
    return lax.broadcasted_iota(I32, shape, dim)


def one_hot(mask):
    return jnp.where(mask, 1.0, 0.0).astype(BF16)


def div12(t):
    return lax.shift_right_logical(t * 171, 11)


def div48(t):
    return jnp.where(t >= 144, 3, jnp.where(t >= 96, 2, jnp.where(t >= 48, 1, 0)))


def band_cells(t, upper, edge):
    slot = jnp.where(t >= ROOM, 1, 0)
    t = t - ROOM * slot
    i = div12(t)
    j = t - WLON * i
    left = (PAD - WLON // 2) + WLON * slot + j
    right = left + 2 * WLON
    if upper:
        usual = i * WIDE + left
        other = (i + HALF) * WIDE + right
        at_edge = jnp.logical_and(edge, i < HALF)
    else:
        usual = i * WIDE + right
        other = (i - HALF) * WIDE + left
        at_edge = jnp.logical_and(edge, i >= HALF)
    return jnp.where(t < SIDE, jnp.where(at_edge, other, usual), -1)


def mean_of(x):
    return jnp.sum(x, axis=-1, keepdims=True) * (1.0 / C)


def norm(x, gain):
    centered = x - mean_of(x)
    rstd = lax.rsqrt(mean_of(centered * centered) + EPS)
    xhat = centered * rstd
    return xhat, rstd, xhat * gain


def norm_back(d_out, xhat, rstd, gain):
    d_hat = d_out * gain
    return rstd * (d_hat - mean_of(d_hat) - xhat * mean_of(d_hat * xhat))


def gelu_parts(u):
    bell = jnp.exp2(u * u * (-0.5 * LOG2E))
    t = 1.0 / (1.0 + (0.3275911 * math.sqrt(0.5)) * jnp.abs(u))
    poly = t * (
        0.5 * 0.254829592
        + t
        * (
            0.5 * -0.284496736
            + t * (0.5 * 1.421413741 + t * (0.5 * -1.453152027 + t * (0.5 * 1.061405429)))
        )
    )
    tail = poly * bell
    cdf = jnp.where(u >= 0, 1.0 - tail, tail)
    return u * cdf, cdf + u * bell * (1.0 / math.sqrt(2.0 * math.pi))


def kernel(
    lats,
    lons,
    tok_hbm,
    g1_hbm,
    wqkv_hbm,
    table_hbm,
    index_hbm,
    region_hbm,
    wproj_hbm,
    g2_hbm,
    fc1_hbm,
    fc2_hbm,
    rec_hbm,
    cot_hbm,
    field_ref,
    grad_ref,
    ext_tok,
    ext_pix,
    back_pix,
    back_grad,
    got_pix_side,
    got_pix_low,
    got_pix_corner,
    got_pix_high,
    got_grad_side,
    got_grad_low,
    got_grad_corner,
    got_grad_high,
    g1_v,
    g2_v,
    wqkv,
    table,
    index,
    region,
    wproj,
    fc1,
    fc2,
    rec,
    cot,
    index_rows,
    index_square,
    bias,
    wsplit,
    local_sem,
    send_sem,
    recv_sem,
):
    lat = lax.axis_index("lat")
    lon = lax.axis_index("lon")
    first = lat == 0
    last = lat == lats - 1
    right = lax.rem(lon + 1, lons)
    left = lax.rem(lon + lons - 1, lons)
    above = lat - 1
    below = lat + 1

    barrier = pltpu.get_barrier_semaphore()

    def greet(row, column):
        pl.semaphore_signal(barrier, inc=1, device_id=(row, column), device_id_type=MESH)

    greet(lat, left)
    greet(lat, right)

    @pl.when(jnp.logical_not(first))
    def _():
        greet(above, lon)
        greet(above, left)

    @pl.when(jnp.logical_not(last))
    def _():
        greet(below, lon)
        greet(below, right)

    def local(src, dst, number):
        copy = pltpu.make_async_copy(src, dst, local_sem.at[number])
        copy.start()
        return copy

    own_copy = local(tok_hbm, ext_tok.at[HALF : HALF + ROWS, PAD:WIDE], 1)
    cot_copy = local(cot_hbm, cot, 0)
    index_copy = local(index_hbm, index, 2)
    table_copy = local(table_hbm.at[pl.ds(lat, 2)], table, 3)
    region_copy = local(region_hbm, region, 4)
    g1_copy = local(g1_hbm, g1_v, 5)
    wqkv_copy = local(wqkv_hbm, wqkv, 6)
    wproj_copy = local(wproj_hbm, wproj, 7)
    g2_copy = local(g2_hbm, g2_v, 8)
    fc1_copy = local(fc1_hbm, fc1, 9)
    fc2_copy = local(fc2_hbm, fc2, 10)
    rec_copy = local(rec_hbm, rec, 11)

    def remote(src, dst, number, row, column):
        return pltpu.make_async_remote_copy(
            src_ref=src,
            dst_ref=dst,
            send_sem=send_sem.at[number],
            recv_sem=recv_sem.at[number],
            device_id=(row, column),
            device_id_type=MESH,
        )

    def outward(src, ext, base):
        side = remote(
            src(slice(0, ROWS), slice(COLS - PAD, COLS)),
            ext.at[HALF : HALF + ROWS, 0:PAD],
            base,
            lat,
            right,
        )
        low = remote(
            src(slice(HALF, ROWS), slice(0, 2 * PAD)),
            ext.at[0:HALF, PAD : 3 * PAD],
            base + 1,
            below,
            lon,
        )
        corner = remote(
            src(slice(HALF, ROWS), slice(COLS - PAD, COLS)),
            ext.at[0:HALF, 0:PAD],
            base + 2,
            below,
            right,
        )
        high = remote(
            src(slice(0, HALF), slice(PAD, COLS)),
            ext.at[HALF + ROWS : TALL, 2 * PAD : WIDE],
            base + 3,
            above,
            lon,
        )
        return side, low, corner, high

    def homeward(ext, side_ref, low_ref, corner_ref, high_ref, base):
        side = remote(ext.at[HALF : HALF + ROWS, 0:PAD], side_ref, base, lat, left)
        low = remote(ext.at[0:HALF, PAD : 3 * PAD], low_ref, base + 1, above, lon)
        corner = remote(ext.at[0:HALF, 0:PAD], corner_ref, base + 2, above, left)
        high = remote(
            ext.at[HALF + ROWS : TALL, 2 * PAD : WIDE], high_ref, base + 3, below, lon
        )
        return side, low, corner, high

    def send(copies, down):
        side, low, corner, high = copies
        goes, comes = (last, first) if down else (first, last)

        @pl.when(jnp.logical_not(goes))
        def _():
            corner.start()
            low.start()

        side.start()

        @pl.when(jnp.logical_not(comes))
        def _():
            high.start()

    def receive(copies, down):
        side, low, corner, high = copies
        goes, comes = (last, first) if down else (first, last)
        side.wait_recv()

        @pl.when(jnp.logical_not(comes))
        def _():
            low.wait_recv()
            corner.wait_recv()

        @pl.when(jnp.logical_not(goes))
        def _():
            high.wait_recv()

    def sent(copies, down):
        side, low, corner, high = copies
        goes, comes = (last, first) if down else (first, last)
        side.wait_send()

        @pl.when(jnp.logical_not(goes))
        def _():
            low.wait_send()
            corner.wait_send()

        @pl.when(jnp.logical_not(comes))
        def _():
            high.wait_send()

    def own_part(ext):
        return lambda a, b: ext.at[
            slice(HALF + a.start, HALF + a.stop), slice(PAD + b.start, PAD + b.stop)
        ]

    out_tok = outward(own_part(ext_tok), ext_tok, 0)

    r_col = iota((4 * COLS, 1), 0)
    j_col = div48(r_col)
    spread = one_hot(iota((4 * COLS, 4 * COLS), 1) == 4 * (r_col - COLS * j_col) + j_col)
    c_row = iota((1, ROWS * PIX), 1)
    a_row = lax.shift_right_logical(c_row, 7)
    vi_row = jnp.bitwise_and(c_row, GROUP - 1)
    v_row = lax.shift_right_logical(vi_row, 2)
    pix_row = jnp.where(
        vi_row < 4 * VARS, v_row * (4 * ROWS) + 4 * a_row + jnp.bitwise_and(vi_row, 3), -1
    )
    place = one_hot(iota((4 * VARS * ROWS, ROWS * PIX), 0) == pix_row)
    j_of_lane = jnp.bitwise_and(lax.shift_right_logical(c_row, 5), 3)

    chosen = []
    chosen_t = []
    for band in range(2):
        edge = first if band == 0 else last
        cells = band_cells(iota((BAND, 1), 0), band == 0, edge)
        chosen.append(one_hot(iota((BAND, WLAT * WIDE), 1) == cells))
        cells = band_cells(iota((1, BAND), 1), band == 0, edge)
        chosen_t.append(one_hot(iota((WLAT * WIDE, BAND), 0) == cells))

    for ext in (ext_tok, ext_pix):
        ext[0:HALF, 3 * PAD : WIDE] = jnp.zeros((HALF, PAD, ext.shape[2]), BF16)
        ext[HALF + ROWS : TALL, 0 : 2 * PAD] = jnp.zeros((HALF, 2 * PAD, ext.shape[2]), BF16)

        @pl.when(first)
        def _():
            ext[0:HALF, 0 : 3 * PAD] = jnp.zeros((HALF, 3 * PAD, ext.shape[2]), BF16)

        @pl.when(last)
        def _():
            ext[HALF + ROWS : TALL, 2 * PAD : WIDE] = jnp.zeros(
                (HALF, 2 * PAD, ext.shape[2]), BF16
            )

    cot_copy.wait()
    pixels = cot[...].astype(F32).reshape(4 * VARS * ROWS, 4 * COLS).astype(BF16)
    by_column = mm_t(spread, pixels).astype(BF16)
    grouped = mm(by_column, place)
    by_token = jnp.zeros((COLS, ROWS * PIX), F32)
    for j in range(4):
        by_token = jnp.where(j_of_lane == j, grouped[j * COLS : (j + 1) * COLS], by_token)
    by_token = by_token.astype(BF16)
    for a in range(ROWS):
        ext_pix[HALF + a, PAD:WIDE, :] = by_token[:, a * PIX : (a + 1) * PIX]

    out_pix = outward(own_part(ext_pix), ext_pix, 4)
    own_copy.wait()
    pl.semaphore_wait(barrier, 6 - 2 * jnp.where(first, 1, 0) - 2 * jnp.where(last, 1, 0))
    send(out_tok, True)
    send(out_pix, True)

    index_copy.wait()
    index_rows[...] = jnp.zeros(index_rows.shape, I32)
    index_square[...] = jnp.zeros(index_square.shape, I32)
    pairs = SIDE * SIDE
    for band in range(2):
        index_rows[band : band + 1, FRONT : FRONT + pairs] = index[pl.ds(lat + band, 1), :]
    for t in range(SIDE):
        start = FRONT + SIDE * t
        usual = index_rows[:, start : start + SIDE]
        upper = usual[0:1]
        lower = usual[1:2]
        if t < SIDE // 2:
            start = FRONT + SIDE * (t + SIDE // 2) + SIDE // 2
            upper = jnp.where(first, index_rows[0:1, start : start + SIDE], upper)
        else:
            start = FRONT + SIDE * (t - SIDE // 2) - SIDE // 2
            lower = jnp.where(last, index_rows[1:2, start : start + SIDE], lower)
        index_square[0, t : t + 1, 0:SIDE] = upper
        index_square[1, t : t + 1, 0:SIDE] = lower

    table_copy.wait()
    region_copy.wait()
    k_col = iota((SIDE, 1), 0)
    q_row = iota((1, LANES), 1)
    i_col = div12(k_col)
    i_row = div12(q_row)
    slot_count = table.shape[2]

    def table_part(band, h, c):
        stop = min(slot_count, (c + 1) * LANES)
        part = table[band, h : h + 1, c * LANES : stop]
        if stop - c * LANES < LANES:
            part = jnp.concatenate(
                [part, jnp.zeros((1, LANES - (stop - c * LANES)), F32)], axis=1
            )
        return part

    for band in range(2):
        code_col = jnp.zeros((SIDE, 1), I32)
        code_row = jnp.zeros((1, LANES), I32)
        for i in range(WLAT):
            row = WLAT * lat - HALF + WLAT * band + i
            if band == 0 and i < HALF:
                row = row + jnp.where(first, HALF, 0)
            if band == 1 and i >= HALF:
                row = row - jnp.where(last, HALF, 0)
            code = region[row]
            if band == 0 and i < HALF:
                code = code + jnp.where(first, 1000, 0)
            if band == 1 and i < HALF:
                code = code + jnp.where(last, 1000, 0)
            code_col = jnp.where(i_col == i, code, code_col)
            code_row = jnp.where(i_row == i, code, code_row)
        allowed = code_col == code_row
        square = index_square[band].T[0:SIDE]
        lane = jnp.bitwise_and(square, LANES - 1)
        chunk = lax.shift_right_logical(square, 7)
        entries = [
            [
                jnp.broadcast_to(table_part(band, h, c), (8, LANES))
                for c in range(-(-slot_count // LANES))
            ]
            for h in range(HEADS)
        ]
        for r in range(0, SIDE, 8):
            for h in range(HEADS):
                picked = jnp.zeros((8, LANES), F32)
                for c, part in enumerate(entries[h]):
                    found = jnp.take_along_axis(
                        part, lane[r : r + 8], axis=1, mode="promise_in_bounds"
                    )
                    picked = jnp.where(chunk[r : r + 8] == c, found, picked)
                bias[band, h, r : r + 8, :] = jnp.where(
                    allowed[r : r + 8], picked * LOG2E, MASKED
                )[:, 0:ROOM]
        for h in range(HEADS):
            bias[band, h, SIDE:ROOM, :] = jnp.full((ROOM - SIDE, ROOM), MASKED, F32)

    def to_windows(ext):
        width = ext.shape[2]
        return jnp.concatenate(
            [
                mm(
                    chosen[band],
                    ext[band * WLAT : (band + 1) * WLAT].reshape(WLAT * WIDE, width),
                )
                for band in range(2)
            ],
            axis=0,
        )

    def to_grid(values, ext):
        width = ext.shape[2]
        for band in range(2):
            ext[band * WLAT : (band + 1) * WLAT] = (
                mm(chosen_t[band], values[band * BAND : (band + 1) * BAND])
                .astype(BF16)
                .reshape(WLAT, WIDE, width)
            )

    g1_copy.wait()
    g2_copy.wait()
    wqkv_copy.wait()
    wproj_copy.wait()
    fc1_copy.wait()
    fc2_copy.wait()
    rec_copy.wait()
    gain1 = g1_v[...].reshape(1, C)
    gain2 = g2_v[...].reshape(1, C)

    c_lane = iota((PIX, 1), 0)
    vi_lane = jnp.bitwise_and(c_lane, GROUP - 1)
    source = (
        16 * lax.shift_right_logical(vi_lane, 2)
        + 4 * jnp.bitwise_and(vi_lane, 3)
        + lax.shift_right_logical(c_lane, 5)
    )
    source = jnp.where(vi_lane < 4 * VARS, source, -1)
    source = one_hot(iota((PIX, 16 * VARS), 1) == source)
    rec_wide = mm(source, rec[...]).astype(BF16)

    head_of_lane = lax.shift_right_logical(iota((1, LANES), 1), 5)
    head_masks = [jnp.where(head_of_lane == h, 1.0, 0.0).astype(BF16) for h in range(4)]

    for n in range(3):
        wsplit[n] = wqkv[:, n * C : (n + 1) * C]
    receive(out_tok, True)
    tokens = to_windows(ext_tok)

    xhat1, rstd1, normed = norm(tokens, gain1)
    normed = normed.astype(BF16)
    wq, wk, wv = wsplit[0], wsplit[1], wsplit[2]
    query = mm(normed, wq).astype(BF16)
    key = mm(normed, wk).astype(BF16)
    value = mm(normed, wv).astype(BF16)

    def lanes_of(x, slot, group):
        low = GROUPS[group][0] * DEPTH
        return x[slot * ROOM : (slot + 1) * ROOM, low : GROUPS[group][1] * DEPTH]

    def stack(x):
        width = x.shape[1]
        return jnp.concatenate([x * head_masks[h][:, 0:width] for h in range(width // DEPTH)])

    def by_head(x):
        heads = x.shape[0] // ROOM
        lane_head = head_of_lane[:, 0 : x.shape[1]]
        out = x[(heads - 1) * ROOM :]
        for h in range(heads - 2, -1, -1):
            out = jnp.where(lane_head == h, x[h * ROOM : (h + 1) * ROOM], out)
        return out

    def join(parts):
        return jnp.concatenate(
            [jnp.concatenate([p.astype(BF16) for p in pair], axis=1) for pair in parts], axis=0
        )

    units = [(slot, group) for slot in range(4) for group in range(len(GROUPS))]
    key_stacks = {u: stack(lanes_of(key, *u)) for u in units}
    scores = {u: mm_t(key_stacks[u], lanes_of(query, *u)) for u in units}
    value_stacks = {u: stack(lanes_of(value, *u)) for u in units}
    kept = {}
    weights = {}
    for slot, group in units:
        parts = []
        for n, h in enumerate(range(*GROUPS[group])):
            s = scores[slot, group][n * ROOM : (n + 1) * ROOM]
            s = s * (SCALE * LOG2E) + bias[slot // 2, h]
            s = jnp.exp2(s - jnp.max(s, axis=0, keepdims=True))
            p = s * (1.0 / jnp.sum(s, axis=0, keepdims=True))
            kept[slot, h] = p
            parts.append(p.astype(BF16))
        weights[slot, group] = jnp.concatenate(parts, axis=0)
    attended = {u: mm_tl(weights[u], value_stacks[u]) for u in units}
    attended = [[attended[slot, 0], attended[slot, 1]] for slot in range(4)]
    attended = join(attended)

    resid = (tokens + mm(attended, wproj[...])).astype(BF16)
    xhat2, rstd2, normed2 = norm(resid.astype(F32), gain2)
    hidden, slope = gelu_parts(mm(normed2.astype(BF16), fc1[...]))
    hidden = hidden.astype(BF16)
    block_out = (resid.astype(F32) + mm_t(hidden, fc2[...])).astype(BF16)
    to_grid(mm_t(block_out, rec_wide).astype(BF16), back_pix)
    home_pix = homeward(
        back_pix, got_pix_side, got_pix_low, got_pix_corner, got_pix_high, 8
    )
    send(home_pix, False)

    receive(out_pix, True)
    d_block = mm(to_windows(ext_pix).astype(BF16), rec_wide).astype(BF16)
    d_hidden = mm(d_block, fc2[...]).astype(BF16).astype(F32)
    d_hidden = (d_hidden * slope).astype(BF16)
    d_normed2 = mm_t(d_hidden, fc1[...]).astype(BF16).astype(F32)
    d_resid = (
        d_block.astype(F32) + norm_back(d_normed2, xhat2, rstd2, gain2).astype(BF16).astype(F32)
    ).astype(BF16)
    d_attended = mm_t(d_resid, wproj[...]).astype(BF16)

    d_outs = {u: lanes_of(d_attended, *u) for u in units}
    d_weights = {u: mm_t(value_stacks[u], d_outs[u]) for u in units}
    d_value = {u: by_head(mm(weights[u], d_outs[u])) for u in units}
    d_scores = {}
    for slot, group in units:
        parts = []
        for n, h in enumerate(range(*GROUPS[group])):
            p = kept[slot, h]
            pd = p * d_weights[slot, group][n * ROOM : (n + 1) * ROOM]
            d = (pd - p * jnp.sum(pd, axis=0, keepdims=True)) * SCALE
            parts.append(d.astype(BF16))
        d_scores[slot, group] = jnp.concatenate(parts, axis=0)
    d_query = {u: mm_tl(d_scores[u], key_stacks[u]) for u in units}
    d_key = {u: by_head(mm(d_scores[u], lanes_of(query, *u))) for u in units}
    d_query, d_key, d_value = (
        [[d[slot, 0], d[slot, 1]] for slot in range(4)] for d in (d_query, d_key, d_value)
    )
    d_query, d_key, d_value = join(d_query), join(d_key), join(d_value)

    d_normed = mm_t(d_query, wq) + mm_t(d_key, wk) + mm_t(d_value, wv)
    d_normed = d_normed.astype(BF16).astype(F32)
    through = norm_back(d_normed, xhat1, rstd1, gain1).astype(BF16).astype(F32)
    to_grid((d_resid.astype(F32) + through).astype(BF16), back_grad)
    home_grad = homeward(
        back_grad, got_grad_side, got_grad_low, got_grad_corner, got_grad_high, 12
    )
    send(home_grad, False)

    def gather_home(ext, side, low, corner, high):
        width = ext.shape[2]
        own = ext[HALF : HALF + ROWS, PAD:WIDE, :].astype(F32)
        from_side = side[...].astype(F32)
        from_low = jnp.where(last, 0.0, low[...].astype(F32))
        from_corner = jnp.where(last, 0.0, corner[...].astype(F32))
        from_high = jnp.where(first, 0.0, high[...].astype(F32))
        upper = jnp.concatenate(
            [
                own[0:HALF, 0:PAD],
                own[0:HALF, PAD : 2 * PAD] + from_high[:, 0:PAD],
                own[0:HALF, 2 * PAD :] + from_high[:, PAD:] + from_side[0:HALF],
            ],
            axis=1,
        )
        lower = jnp.concatenate(
            [
                own[HALF:, 0 : 2 * PAD] + from_low,
                own[HALF:, 2 * PAD :] + from_corner + from_side[HALF:],
            ],
            axis=1,
        )
        return jnp.concatenate([upper, lower], axis=0)

    receive(home_pix, False)
    patches = gather_home(
        back_pix, got_pix_side, got_pix_low, got_pix_corner, got_pix_high
    )
    patches = jnp.concatenate([patches[a] for a in range(ROWS)], axis=1)
    patches = jnp.concatenate(
        [jnp.where(j_of_lane == j, patches, 0.0) for j in range(4)], axis=0
    ).astype(BF16)
    by_pixel = mm_t(place, patches).astype(BF16)
    field = mm(by_pixel, spread)
    field_ref[...] = field.reshape(VARS, 4 * ROWS, 4 * COLS).astype(BF16)

    receive(home_grad, False)
    grad_ref[...] = gather_home(
        back_grad, got_grad_side, got_grad_low, got_grad_corner, got_grad_high
    ).astype(BF16)

    sent(out_tok, True)
    sent(out_pix, True)
    sent(home_pix, False)
    sent(home_grad, False)


def put_kernel(a_ref, b_ref, a_out, b_out, sem):
    copies = [
        pltpu.make_async_copy(a_ref, a_out, sem.at[0]),
        pltpu.make_async_copy(b_ref, b_out, sem.at[1]),
    ]
    for copy in copies:
        copy.start()
    for copy in copies:
        copy.wait()


def put(a, b):
    return pl.pallas_call(
        put_kernel,
        out_shape=(pltpu.HBM(a.shape, a.dtype), pltpu.HBM(b.shape, b.dtype)),
        in_specs=[pl.BlockSpec(memory_space=pltpu.VMEM)] * 2,
        out_specs=(pl.BlockSpec(memory_space=pl.ANY), pl.BlockSpec(memory_space=pl.ANY)),
        scratch_shapes=[pltpu.SemaphoreType.DMA((2,))],
    )(pltpu.with_memory_space_constraint(a, pltpu.VMEM), pltpu.with_memory_space_constraint(b, pltpu.VMEM))


def per_device(lats, lons, *args):
    tokens, _, _, table, index, region = args[:6]
    cot = args[-1]
    operands = (*args[:9], args[9].T, args[10].T, cot)
    scratch = [
        pltpu.VMEM((TALL, WIDE, C), BF16),
        pltpu.VMEM((TALL, WIDE, PIX), BF16),
        pltpu.VMEM((TALL, WIDE, PIX), BF16),
        pltpu.VMEM((TALL, WIDE, C), BF16),
    ]
    for width in (PIX, C):
        scratch += [
            pltpu.VMEM((ROWS, PAD, width), BF16),
            pltpu.VMEM((HALF, 2 * PAD, width), BF16),
            pltpu.VMEM((HALF, PAD, width), BF16),
            pltpu.VMEM((HALF, 2 * PAD, width), BF16),
        ]
    scratch += [
        pltpu.VMEM((C,), F32),
        pltpu.VMEM((C,), F32),
        pltpu.VMEM((C, 3 * C), BF16),
        pltpu.VMEM((2,) + table.shape[1:], F32),
        pltpu.VMEM(index.shape, I32),
        pltpu.SMEM(region.shape, I32),
        pltpu.VMEM((C, C), BF16),
        pltpu.VMEM((C, MLP), BF16),
        pltpu.VMEM((C, MLP), BF16),
        pltpu.VMEM((16 * VARS, C), BF16),
        pltpu.VMEM(cot.shape, BF16),
        pltpu.VMEM((2, FRONT + 41 * LANES + LANES), I32),
        pltpu.VMEM((2, LANES, LANES), I32),
        pltpu.VMEM((2, HEADS, ROOM, ROOM), F32),
        pltpu.VMEM((3, C, C), BF16),
        pltpu.SemaphoreType.DMA((12,)),
        pltpu.SemaphoreType.DMA((16,)),
        pltpu.SemaphoreType.DMA((16,)),
    ]
    field, grad = pl.pallas_call(
        functools.partial(kernel, lats, lons),
        out_shape=(
            pltpu.VMEM(cot.shape, BF16),
            pltpu.VMEM(tokens.shape, BF16),
        ),
        in_specs=[pl.BlockSpec(memory_space=pltpu.HBM)] * 12,
        out_specs=(
            pl.BlockSpec(memory_space=pltpu.VMEM),
            pl.BlockSpec(memory_space=pltpu.VMEM),
        ),
        scratch_shapes=scratch,
        compiler_params=pltpu.CompilerParams(
            collective_id=0, has_side_effects=True, vmem_limit_bytes=40 * 1024 * 1024
        ),
    )(*(pltpu.with_memory_space_constraint(x, pltpu.HBM) for x in operands))
    return put(field, grad)


def solution(mesh):
    return jax.shard_map(
        functools.partial(per_device, mesh.shape["lat"], mesh.shape["lon"]),
        mesh=mesh,
        in_specs=(P("lat", "lon", None),) + (P(),) * 10 + (P(None, "lat", "lon"),),
        out_specs=(P(None, "lat", "lon"), P("lat", "lon", None)),
        check_vma=False,
    )
```

```python
import functools
import math

import jax
import jax.numpy as jnp
from jax import lax
from jax.experimental import pallas as pl
from jax.experimental.pallas import tpu as pltpu
from jax.sharding import PartitionSpec as P

F32 = jnp.float32
BF16 = jnp.bfloat16
I32 = jnp.int32
MESH = pl.DeviceIdType.MESH

WLAT = 6
WLON = 12
SIDE = WLAT * WLON
ROOM = 80
HEADS = 6
DEPTH = 32
C = HEADS * DEPTH
MLP = 768
VARS = 5
ROWS = 6
COLS = 48
HALF = WLAT // 2
PAD = 16
WIDE = COLS + PAD
TALL = 2 * WLAT
SLOTS_PER_BAND = 2
BAND = SLOTS_PER_BAND * ROOM
TOKENS = 2 * BAND
LANES = 128
GROUP = 32
PIX = 4 * GROUP
EPS = 1e-05
LOG2E = math.log2(math.e)
SCALE = 1.0 / math.sqrt(DEPTH)
MASKED = -1.0e9
FRONT = LANES
GROUPS = ((0, 4), (4, 6))


def mm(a, b):
    return lax.dot_general(a, b, (((1,), (0,)), ((), ())), preferred_element_type=F32)


def mm_t(a, b):
    return lax.dot_general(a, b, (((1,), (1,)), ((), ())), preferred_element_type=F32)


def mm_tl(a, b):
    return lax.dot_general(a, b, (((0,), (0,)), ((), ())), preferred_element_type=F32)


def iota(shape, dim):
    return lax.broadcasted_iota(I32, shape, dim)


def one_hot(mask):
    return jnp.where(mask, 1.0, 0.0).astype(BF16)


def div12(t):
    return lax.shift_right_logical(t * 171, 11)


def div48(t):
    return jnp.where(t >= 144, 3, jnp.where(t >= 96, 2, jnp.where(t >= 48, 1, 0)))


def band_cells(t, upper, edge):
    slot = jnp.where(t >= ROOM, 1, 0)
    t = t - ROOM * slot
    i = div12(t)
    j = t - WLON * i
    left = (PAD - WLON // 2) + WLON * slot + j
    right = left + 2 * WLON
    if upper:
        usual = i * WIDE + left
        other = (i + HALF) * WIDE + right
        at_edge = jnp.logical_and(edge, i < HALF)
    else:
        usual = i * WIDE + right
        other = (i - HALF) * WIDE + left
        at_edge = jnp.logical_and(edge, i >= HALF)
    return jnp.where(t < SIDE, jnp.where(at_edge, other, usual), -1)


def mean_of(x):
    return jnp.sum(x, axis=-1, keepdims=True) * (1.0 / C)


def norm(x, gain):
    centered = x - mean_of(x)
    rstd = lax.rsqrt(mean_of(centered * centered) + EPS)
    xhat = centered * rstd
    return xhat, rstd, xhat * gain


def norm_back(d_out, xhat, rstd, gain):
    d_hat = d_out * gain
    return rstd * (d_hat - mean_of(d_hat) - xhat * mean_of(d_hat * xhat))


def gelu_parts(u):
    bell = jnp.exp2(u * u * (-0.5 * LOG2E))
    t = 1.0 / (1.0 + (0.3275911 * math.sqrt(0.5)) * jnp.abs(u))
    poly = t * (
        0.5 * 0.254829592
        + t
        * (
            0.5 * -0.284496736
            + t * (0.5 * 1.421413741 + t * (0.5 * -1.453152027 + t * (0.5 * 1.061405429)))
        )
    )
    tail = poly * bell
    cdf = jnp.where(u >= 0, 1.0 - tail, tail)
    return u * cdf, cdf + u * bell * (1.0 / math.sqrt(2.0 * math.pi))


def kernel(
    lats,
    lons,
    tok_hbm,
    g1_hbm,
    wqkv_hbm,
    table_hbm,
    index_hbm,
    region_hbm,
    wproj_hbm,
    g2_hbm,
    fc1_hbm,
    fc2_hbm,
    rec_hbm,
    cot_hbm,
    field_ref,
    grad_ref,
    ext_tok,
    ext_pix,
    back_pix,
    back_grad,
    got_pix_side,
    got_pix_low,
    got_pix_corner,
    got_pix_high,
    got_grad_side,
    got_grad_low,
    got_grad_corner,
    got_grad_high,
    g1_v,
    g2_v,
    wqkv,
    table,
    index,
    region,
    wproj,
    fc1,
    fc2,
    rec,
    cot,
    index_rows,
    index_square,
    bias,
    wsplit,
    local_sem,
    send_sem,
    recv_sem,
):
    lat = lax.axis_index("lat")
    lon = lax.axis_index("lon")
    first = lat == 0
    last = lat == lats - 1
    right = lax.rem(lon + 1, lons)
    left = lax.rem(lon + lons - 1, lons)
    above = lat - 1
    below = lat + 1

    barrier = pltpu.get_barrier_semaphore()

    def greet(row, column):
        pl.semaphore_signal(barrier, inc=1, device_id=(row, column), device_id_type=MESH)

    greet(lat, left)
    greet(lat, right)

    @pl.when(jnp.logical_not(first))
    def _():
        greet(above, lon)
        greet(above, left)

    @pl.when(jnp.logical_not(last))
    def _():
        greet(below, lon)
        greet(below, right)

    def local(src, dst, number):
        copy = pltpu.make_async_copy(src, dst, local_sem.at[number])
        copy.start()
        return copy

    own_copy = local(tok_hbm, ext_tok.at[HALF : HALF + ROWS, PAD:WIDE], 1)
    cot_copy = local(cot_hbm, cot, 0)
    index_copy = local(index_hbm, index, 2)
    table_copy = local(table_hbm.at[pl.ds(lat, 2)], table, 3)
    region_copy = local(region_hbm, region, 4)
    g1_copy = local(g1_hbm, g1_v, 5)
    wqkv_copy = local(wqkv_hbm, wqkv, 6)
    wproj_copy = local(wproj_hbm, wproj, 7)
    g2_copy = local(g2_hbm, g2_v, 8)
    fc1_copy = local(fc1_hbm, fc1, 9)
    fc2_copy = local(fc2_hbm, fc2, 10)
    rec_copy = local(rec_hbm, rec, 11)

    def remote(src, dst, number, row, column):
        return pltpu.make_async_remote_copy(
            src_ref=src,
            dst_ref=dst,
            send_sem=send_sem.at[number],
            recv_sem=recv_sem.at[number],
            device_id=(row, column),
            device_id_type=MESH,
        )

    def outward(src, ext, base):
        side = remote(
            src(slice(0, ROWS), slice(COLS - PAD, COLS)),
            ext.at[HALF : HALF + ROWS, 0:PAD],
            base,
            lat,
            right,
        )
        low = remote(
            src(slice(HALF, ROWS), slice(0, 2 * PAD)),
            ext.at[0:HALF, PAD : 3 * PAD],
            base + 1,
            below,
            lon,
        )
        corner = remote(
            src(slice(HALF, ROWS), slice(COLS - PAD, COLS)),
            ext.at[0:HALF, 0:PAD],
            base + 2,
            below,
            right,
        )
        high = remote(
            src(slice(0, HALF), slice(PAD, COLS)),
            ext.at[HALF + ROWS : TALL, 2 * PAD : WIDE],
            base + 3,
            above,
            lon,
        )
        return side, low, corner, high

    def homeward(ext, side_ref, low_ref, corner_ref, high_ref, base):
        side = remote(ext.at[HALF : HALF + ROWS, 0:PAD], side_ref, base, lat, left)
        low = remote(ext.at[0:HALF, PAD : 3 * PAD], low_ref, base + 1, above, lon)
        corner = remote(ext.at[0:HALF, 0:PAD], corner_ref, base + 2, above, left)
        high = remote(
            ext.at[HALF + ROWS : TALL, 2 * PAD : WIDE], high_ref, base + 3, below, lon
        )
        return side, low, corner, high

    def send(copies, down):
        side, low, corner, high = copies
        goes, comes = (last, first) if down else (first, last)

        @pl.when(jnp.logical_not(goes))
        def _():
            corner.start()
            low.start()

        side.start()

        @pl.when(jnp.logical_not(comes))
        def _():
            high.start()

    def receive(copies, down):
        side, low, corner, high = copies
        goes, comes = (last, first) if down else (first, last)
        side.wait_recv()

        @pl.when(jnp.logical_not(comes))
        def _():
            low.wait_recv()
            corner.wait_recv()

        @pl.when(jnp.logical_not(goes))
        def _():
            high.wait_recv()

    def sent(copies, down):
        side, low, corner, high = copies
        goes, comes = (last, first) if down else (first, last)
        side.wait_send()

        @pl.when(jnp.logical_not(goes))
        def _():
            low.wait_send()
            corner.wait_send()

        @pl.when(jnp.logical_not(comes))
        def _():
            high.wait_send()

    def own_part(ext):
        return lambda a, b: ext.at[
            slice(HALF + a.start, HALF + a.stop), slice(PAD + b.start, PAD + b.stop)
        ]

    out_tok = outward(own_part(ext_tok), ext_tok, 0)

    r_col = iota((4 * COLS, 1), 0)
    j_col = div48(r_col)
    spread = one_hot(iota((4 * COLS, 4 * COLS), 1) == 4 * (r_col - COLS * j_col) + j_col)
    c_row = iota((1, ROWS * PIX), 1)
    a_row = lax.shift_right_logical(c_row, 7)
    vi_row = jnp.bitwise_and(c_row, GROUP - 1)
    v_row = lax.shift_right_logical(vi_row, 2)
    pix_row = jnp.where(
        vi_row < 4 * VARS, v_row * (4 * ROWS) + 4 * a_row + jnp.bitwise_and(vi_row, 3), -1
    )
    place = one_hot(iota((4 * VARS * ROWS, ROWS * PIX), 0) == pix_row)
    j_of_lane = jnp.bitwise_and(lax.shift_right_logical(c_row, 5), 3)

    chosen = []
    chosen_t = []
    for band in range(2):
        edge = first if band == 0 else last
        cells = band_cells(iota((BAND, 1), 0), band == 0, edge)
        chosen.append(one_hot(iota((BAND, WLAT * WIDE), 1) == cells))
        cells = band_cells(iota((1, BAND), 1), band == 0, edge)
        chosen_t.append(one_hot(iota((WLAT * WIDE, BAND), 0) == cells))

    for ext in (ext_tok, ext_pix):
        ext[0:HALF, 3 * PAD : WIDE] = jnp.zeros((HALF, PAD, ext.shape[2]), BF16)
        ext[HALF + ROWS : TALL, 0 : 2 * PAD] = jnp.zeros((HALF, 2 * PAD, ext.shape[2]), BF16)

        @pl.when(first)
        def _():
            ext[0:HALF, 0 : 3 * PAD] = jnp.zeros((HALF, 3 * PAD, ext.shape[2]), BF16)

        @pl.when(last)
        def _():
            ext[HALF + ROWS : TALL, 2 * PAD : WIDE] = jnp.zeros(
                (HALF, 2 * PAD, ext.shape[2]), BF16
            )

    cot_copy.wait()
    pixels = cot[...].astype(F32).reshape(4 * VARS * ROWS, 4 * COLS).astype(BF16)
    by_column = mm_t(spread, pixels).astype(BF16)
    grouped = mm(by_column, place)
    by_token = jnp.zeros((COLS, ROWS * PIX), F32)
    for j in range(4):
        by_token = jnp.where(j_of_lane == j, grouped[j * COLS : (j + 1) * COLS], by_token)
    by_token = by_token.astype(BF16)
    for a in range(ROWS):
        ext_pix[HALF + a, PAD:WIDE, :] = by_token[:, a * PIX : (a + 1) * PIX]

    out_pix = outward(own_part(ext_pix), ext_pix, 4)
    own_copy.wait()
    pl.semaphore_wait(barrier, 6 - 2 * jnp.where(first, 1, 0) - 2 * jnp.where(last, 1, 0))
    send(out_tok, True)
    send(out_pix, True)

    index_copy.wait()
    index_rows[...] = jnp.zeros(index_rows.shape, I32)
    index_square[...] = jnp.zeros(index_square.shape, I32)
    pairs = SIDE * SIDE
    for band in range(2):
        index_rows[band : band + 1, FRONT : FRONT + pairs] = index[pl.ds(lat + band, 1), :]
    for t in range(SIDE):
        start = FRONT + SIDE * t
        usual = index_rows[:, start : start + SIDE]
        upper = usual[0:1]
        lower = usual[1:2]
        if t < SIDE // 2:
            start = FRONT + SIDE * (t + SIDE // 2) + SIDE // 2
            upper = jnp.where(first, index_rows[0:1, start : start + SIDE], upper)
        else:
            start = FRONT + SIDE * (t - SIDE // 2) - SIDE // 2
            lower = jnp.where(last, index_rows[1:2, start : start + SIDE], lower)
        index_square[0, t : t + 1, 0:SIDE] = upper
        index_square[1, t : t + 1, 0:SIDE] = lower

    table_copy.wait()
    region_copy.wait()
    k_col = iota((SIDE, 1), 0)
    q_row = iota((1, LANES), 1)
    i_col = div12(k_col)
    i_row = div12(q_row)
    slot_count = table.shape[2]

    def table_part(band, h, c):
        stop = min(slot_count, (c + 1) * LANES)
        part = table[band, h : h + 1, c * LANES : stop]
        if stop - c * LANES < LANES:
            part = jnp.concatenate(
                [part, jnp.zeros((1, LANES - (stop - c * LANES)), F32)], axis=1
            )
        return part

    for band in range(2):
        code_col = jnp.zeros((SIDE, 1), I32)
        code_row = jnp.zeros((1, LANES), I32)
        for i in range(WLAT):
            row = WLAT * lat - HALF + WLAT * band + i
            if band == 0 and i < HALF:
                row = row + jnp.where(first, HALF, 0)
            if band == 1 and i >= HALF:
                row = row - jnp.where(last, HALF, 0)
            code = region[row]
            if band == 0 and i < HALF:
                code = code + jnp.where(first, 1000, 0)
            if band == 1 and i < HALF:
                code = code + jnp.where(last, 1000, 0)
            code_col = jnp.where(i_col == i, code, code_col)
            code_row = jnp.where(i_row == i, code, code_row)
        allowed = code_col == code_row
        square = index_square[band].T[0:SIDE]
        lane = jnp.bitwise_and(square, LANES - 1)
        chunk = lax.shift_right_logical(square, 7)
        entries = [
            [
                jnp.broadcast_to(table_part(band, h, c), (8, LANES))
                for c in range(-(-slot_count // LANES))
            ]
            for h in range(HEADS)
        ]
        for r in range(0, SIDE, 8):
            for h in range(HEADS):
                picked = jnp.zeros((8, LANES), F32)
                for c, part in enumerate(entries[h]):
                    found = jnp.take_along_axis(
                        part, lane[r : r + 8], axis=1, mode="promise_in_bounds"
                    )
                    picked = jnp.where(chunk[r : r + 8] == c, found, picked)
                bias[band, h, r : r + 8, :] = jnp.where(
                    allowed[r : r + 8], picked * LOG2E, MASKED
                )[:, 0:ROOM]
        for h in range(HEADS):
            bias[band, h, SIDE:ROOM, :] = jnp.full((ROOM - SIDE, ROOM), MASKED, F32)

    def to_windows(ext):
        width = ext.shape[2]
        return jnp.concatenate(
            [
                mm(
                    chosen[band],
                    ext[band * WLAT : (band + 1) * WLAT].reshape(WLAT * WIDE, width),
                )
                for band in range(2)
            ],
            axis=0,
        )

    def to_grid(values, ext):
        width = ext.shape[2]
        for band in range(2):
            ext[band * WLAT : (band + 1) * WLAT] = (
                mm(chosen_t[band], values[band * BAND : (band + 1) * BAND])
                .astype(BF16)
                .reshape(WLAT, WIDE, width)
            )

    g1_copy.wait()
    g2_copy.wait()
    wqkv_copy.wait()
    wproj_copy.wait()
    fc1_copy.wait()
    fc2_copy.wait()
    rec_copy.wait()
    gain1 = g1_v[...].reshape(1, C)
    gain2 = g2_v[...].reshape(1, C)

    c_lane = iota((PIX, 1), 0)
    vi_lane = jnp.bitwise_and(c_lane, GROUP - 1)
    source = (
        16 * lax.shift_right_logical(vi_lane, 2)
        + 4 * jnp.bitwise_and(vi_lane, 3)
        + lax.shift_right_logical(c_lane, 5)
    )
    source = jnp.where(vi_lane < 4 * VARS, source, -1)
    source = one_hot(iota((PIX, 16 * VARS), 1) == source)
    rec_wide = mm(source, rec[...]).astype(BF16)

    head_of_lane = lax.shift_right_logical(iota((1, LANES), 1), 5)
    head_masks = [jnp.where(head_of_lane == h, 1.0, 0.0).astype(BF16) for h in range(4)]

    for n in range(3):
        wsplit[n] = wqkv[:, n * C : (n + 1) * C]
    receive(out_tok, True)
    receive(out_pix, True)
    tokens = to_windows(ext_tok)

    xhat1, rstd1, normed = norm(tokens, gain1)
    normed = normed.astype(BF16)
    wq, wk, wv = wsplit[0], wsplit[1], wsplit[2]
    query = mm(normed, wq).astype(BF16)
    key = mm(normed, wk).astype(BF16)
    value = mm(normed, wv).astype(BF16)

    def lanes_of(x, slot, group):
        low = GROUPS[group][0] * DEPTH
        return x[slot * ROOM : (slot + 1) * ROOM, low : GROUPS[group][1] * DEPTH]

    def stack(x):
        width = x.shape[1]
        return jnp.concatenate([x * head_masks[h][:, 0:width] for h in range(width // DEPTH)])

    def by_head(x):
        heads = x.shape[0] // ROOM
        lane_head = head_of_lane[:, 0 : x.shape[1]]
        out = x[(heads - 1) * ROOM :]
        for h in range(heads - 2, -1, -1):
            out = jnp.where(lane_head == h, x[h * ROOM : (h + 1) * ROOM], out)
        return out

    def join(parts):
        return jnp.concatenate(
            [jnp.concatenate([p.astype(BF16) for p in pair], axis=1) for pair in parts], axis=0
        )

    units = [(slot, group) for slot in range(4) for group in range(len(GROUPS))]
    key_stacks = {u: stack(lanes_of(key, *u)) for u in units}
    scores = {u: mm_t(key_stacks[u], lanes_of(query, *u)) for u in units}
    value_stacks = {u: stack(lanes_of(value, *u)) for u in units}
    kept = {}
    weights = {}
    for slot, group in units:
        parts = []
        for n, h in enumerate(range(*GROUPS[group])):
            s = scores[slot, group][n * ROOM : (n + 1) * ROOM]
            s = s * (SCALE * LOG2E) + bias[slot // 2, h]
            s = jnp.exp2(s - jnp.max(s, axis=0, keepdims=True))
            p = s * (1.0 / jnp.sum(s, axis=0, keepdims=True))
            kept[slot, h] = p
            parts.append(p.astype(BF16))
        weights[slot, group] = jnp.concatenate(parts, axis=0)
    attended = {u: mm_tl(weights[u], value_stacks[u]) for u in units}
    attended = [[attended[slot, 0], attended[slot, 1]] for slot in range(4)]
    attended = join(attended)

    resid = (tokens + mm(attended, wproj[...])).astype(BF16)
    xhat2, rstd2, normed2 = norm(resid.astype(F32), gain2)
    hidden, slope = gelu_parts(mm(normed2.astype(BF16), fc1[...]))
    hidden = hidden.astype(BF16)
    block_out = (resid.astype(F32) + mm_t(hidden, fc2[...])).astype(BF16)
    to_grid(mm_t(block_out, rec_wide).astype(BF16), back_pix)
    home_pix = homeward(
        back_pix, got_pix_side, got_pix_low, got_pix_corner, got_pix_high, 8
    )

    d_block = mm(to_windows(ext_pix).astype(BF16), rec_wide).astype(BF16)
    d_hidden = mm(d_block, fc2[...]).astype(BF16).astype(F32)
    d_hidden = (d_hidden * slope).astype(BF16)
    d_normed2 = mm_t(d_hidden, fc1[...]).astype(BF16).astype(F32)
    d_resid = (
        d_block.astype(F32) + norm_back(d_normed2, xhat2, rstd2, gain2).astype(BF16).astype(F32)
    ).astype(BF16)
    d_attended = mm_t(d_resid, wproj[...]).astype(BF16)

    send(home_pix, False)

    d_outs = {u: lanes_of(d_attended, *u) for u in units}
    d_weights = {u: mm_t(value_stacks[u], d_outs[u]) for u in units}
    d_value = {u: by_head(mm(weights[u], d_outs[u])) for u in units}
    d_scores = {}
    for slot, group in units:
        parts = []
        for n, h in enumerate(range(*GROUPS[group])):
            p = kept[slot, h]
            pd = p * d_weights[slot, group][n * ROOM : (n + 1) * ROOM]
            d = (pd - p * jnp.sum(pd, axis=0, keepdims=True)) * SCALE
            parts.append(d.astype(BF16))
        d_scores[slot, group] = jnp.concatenate(parts, axis=0)
    d_query = {u: mm_tl(d_scores[u], key_stacks[u]) for u in units}
    d_key = {u: by_head(mm(d_scores[u], lanes_of(query, *u))) for u in units}
    d_query, d_key, d_value = (
        [[d[slot, 0], d[slot, 1]] for slot in range(4)] for d in (d_query, d_key, d_value)
    )
    d_query, d_key, d_value = join(d_query), join(d_key), join(d_value)

    d_normed = mm_t(d_query, wq) + mm_t(d_key, wk) + mm_t(d_value, wv)
    d_normed = d_normed.astype(BF16).astype(F32)
    through = norm_back(d_normed, xhat1, rstd1, gain1).astype(BF16).astype(F32)
    to_grid((d_resid.astype(F32) + through).astype(BF16), back_grad)
    home_grad = homeward(
        back_grad, got_grad_side, got_grad_low, got_grad_corner, got_grad_high, 12
    )
    send(home_grad, False)

    def gather_home(ext, side, low, corner, high):
        width = ext.shape[2]
        own = ext[HALF : HALF + ROWS, PAD:WIDE, :].astype(F32)
        from_side = side[...].astype(F32)
        from_low = jnp.where(last, 0.0, low[...].astype(F32))
        from_corner = jnp.where(last, 0.0, corner[...].astype(F32))
        from_high = jnp.where(first, 0.0, high[...].astype(F32))
        upper = jnp.concatenate(
            [
                own[0:HALF, 0:PAD],
                own[0:HALF, PAD : 2 * PAD] + from_high[:, 0:PAD],
                own[0:HALF, 2 * PAD :] + from_high[:, PAD:] + from_side[0:HALF],
            ],
            axis=1,
        )
        lower = jnp.concatenate(
            [
                own[HALF:, 0 : 2 * PAD] + from_low,
                own[HALF:, 2 * PAD :] + from_corner + from_side[HALF:],
            ],
            axis=1,
        )
        return jnp.concatenate([upper, lower], axis=0)

    receive(home_pix, False)
    patches = gather_home(
        back_pix, got_pix_side, got_pix_low, got_pix_corner, got_pix_high
    )
    patches = jnp.concatenate([patches[a] for a in range(ROWS)], axis=1)
    patches = jnp.concatenate(
        [jnp.where(j_of_lane == j, patches, 0.0) for j in range(4)], axis=0
    ).astype(BF16)
    by_pixel = mm_t(place, patches).astype(BF16)
    field = mm(by_pixel, spread)
    field_ref[...] = field.reshape(VARS, 4 * ROWS, 4 * COLS).astype(BF16)

    receive(home_grad, False)
    grad_ref[...] = gather_home(
        back_grad, got_grad_side, got_grad_low, got_grad_corner, got_grad_high
    ).astype(BF16)

    sent(out_tok, True)
    sent(out_pix, True)
    sent(home_pix, False)
    sent(home_grad, False)


def put_kernel(a_ref, b_ref, a_out, b_out, sem):
    copies = [
        pltpu.make_async_copy(a_ref, a_out, sem.at[0]),
        pltpu.make_async_copy(b_ref, b_out, sem.at[1]),
    ]
    for copy in copies:
        copy.start()
    for copy in copies:
        copy.wait()


def put(a, b):
    return pl.pallas_call(
        put_kernel,
        out_shape=(pltpu.HBM(a.shape, a.dtype), pltpu.HBM(b.shape, b.dtype)),
        in_specs=[pl.BlockSpec(memory_space=pltpu.VMEM)] * 2,
        out_specs=(pl.BlockSpec(memory_space=pl.ANY), pl.BlockSpec(memory_space=pl.ANY)),
        scratch_shapes=[pltpu.SemaphoreType.DMA((2,))],
    )(pltpu.with_memory_space_constraint(a, pltpu.VMEM), pltpu.with_memory_space_constraint(b, pltpu.VMEM))


def per_device(lats, lons, *args):
    tokens, _, _, table, index, region = args[:6]
    cot = args[-1]
    operands = (*args[:9], args[9].T, args[10].T, cot)
    scratch = [
        pltpu.VMEM((TALL, WIDE, C), BF16),
        pltpu.VMEM((TALL, WIDE, PIX), BF16),
        pltpu.VMEM((TALL, WIDE, PIX), BF16),
        pltpu.VMEM((TALL, WIDE, C), BF16),
    ]
    for width in (PIX, C):
        scratch += [
            pltpu.VMEM((ROWS, PAD, width), BF16),
            pltpu.VMEM((HALF, 2 * PAD, width), BF16),
            pltpu.VMEM((HALF, PAD, width), BF16),
            pltpu.VMEM((HALF, 2 * PAD, width), BF16),
        ]
    scratch += [
        pltpu.VMEM((C,), F32),
        pltpu.VMEM((C,), F32),
        pltpu.VMEM((C, 3 * C), BF16),
        pltpu.VMEM((2,) + table.shape[1:], F32),
        pltpu.VMEM(index.shape, I32),
        pltpu.SMEM(region.shape, I32),
        pltpu.VMEM((C, C), BF16),
        pltpu.VMEM((C, MLP), BF16),
        pltpu.VMEM((C, MLP), BF16),
        pltpu.VMEM((16 * VARS, C), BF16),
        pltpu.VMEM(cot.shape, BF16),
        pltpu.VMEM((2, FRONT + 41 * LANES + LANES), I32),
        pltpu.VMEM((2, LANES, LANES), I32),
        pltpu.VMEM((2, HEADS, ROOM, ROOM), F32),
        pltpu.VMEM((3, C, C), BF16),
        pltpu.SemaphoreType.DMA((12,)),
        pltpu.SemaphoreType.DMA((16,)),
        pltpu.SemaphoreType.DMA((16,)),
    ]
    field, grad = pl.pallas_call(
        functools.partial(kernel, lats, lons),
        out_shape=(
            pltpu.VMEM(cot.shape, BF16),
            pltpu.VMEM(tokens.shape, BF16),
        ),
        in_specs=[pl.BlockSpec(memory_space=pltpu.HBM)] * 12,
        out_specs=(
            pl.BlockSpec(memory_space=pltpu.VMEM),
            pl.BlockSpec(memory_space=pltpu.VMEM),
        ),
        scratch_shapes=scratch,
        compiler_params=pltpu.CompilerParams(
            collective_id=0, has_side_effects=True, vmem_limit_bytes=40 * 1024 * 1024
        ),
    )(*(pltpu.with_memory_space_constraint(x, pltpu.HBM) for x in operands))
    return put(field, grad)


def solution(mesh):
    return jax.shard_map(
        functools.partial(per_device, mesh.shape["lat"], mesh.shape["lon"]),
        mesh=mesh,
        in_specs=(P("lat", "lon", None),) + (P(),) * 10 + (P(None, "lat", "lon"),),
        out_specs=(P(None, "lat", "lon"), P("lat", "lon", None)),
        check_vma=False,
    )
```
